128 devices in a mesh: dp: 2 (over core), expert: 64 (over z, y, x).
Axes of the slice: x: 4, y: 4, z: 4, core: 2. Of those that a mesh axis runs over, the one named last changes fastest.
Arguments:
- tokens: bfloat16 [16384, 4096], P(('dp', 'expert')), may hold values from -6 to 6
- cotangent: bfloat16 [16384, 4096], P(('dp', 'expert')), may hold values from -6 to 6
- routing: int32 [16384, 2], P(('dp', 'expert')), may hold values from 0 to 63, as said below
- combine_weights: float32 [16384, 2], P(('dp', 'expert')), may hold values from 0.05 to 0.3
- w_gate: bfloat16 [64, 4096, 768], P('expert', None, 'dp'), may hold values from -0.09375 to 0.09375
- w_up: bfloat16 [64, 4096, 768], P('expert', None, 'dp'), may hold values from -0.09375 to 0.09375
- w_down: bfloat16 [64, 768, 4096], P('expert', 'dp'), may hold values from -0.21875 to 0.21875
Outputs:
- combined: bfloat16 [16384, 4096], P(('dp', 'expert'))
- token_grad: bfloat16 [16384, 4096], P(('dp', 'expert'))
- gate_weight_grad: bfloat16 [64, 4096, 768], P('expert', None, 'dp')
- up_weight_grad: bfloat16 [64, 4096, 768], P('expert', None, 'dp')
- down_weight_grad: bfloat16 [64, 768, 4096], P('expert', 'dp')
The draws below stay inside these ranges and needn't reach their ends.
Inputs may be any that keep to these rules, and one draw needn't show every extreme that they name: `routing`: each row names 2 different experts. The same 4 experts are named by exactly 8 of the 128 rows of every device; each of the other 60 experts is named by 3 or 4 rows of every device.
All inputs are finite; a program needn't handle non-finite values.
Results may differ from the reference program's by a relative error of at most 0.0065.
Values may be sent and summed in bfloat16 or wider, within the bound.
No kernel may reach another device: no remote copies, remote signals or barrier semaphores. Data moves between devices by JAX's collectives and lax.ppermute only.
A program may use at most 256 MiB of HBM per device.

```python
import jax
import jax.numpy as jnp
from jax import lax

D = 4096
HID = 768
TOPK = 2
HOT = 4
TOK_DEV = 128
EXPERTS = 64
TOKENS = 16384
CAP_HOT = 8
CAP_COLD = 4
CAP = 8


def draw_routing(key, part):
    key = jax.random.fold_in(key, 7)
    hot_key, cold_key, row_key, col_key = jax.random.split(key, 4)
    ranked = jax.random.permutation(hot_key, EXPERTS).astype(jnp.int32)
    hot_set = ranked[:HOT]
    cold_set = ranked[HOT:]
    cold_count = EXPERTS - HOT
    hot_rows = HOT * CAP_HOT
    blocks = TOKENS // TOK_DEV
    row_ids = jnp.arange(TOK_DEV, dtype=jnp.int32)
    col_ids = jnp.arange(TOPK, dtype=jnp.int32)
    has_hot = row_ids < hot_rows
    start = row_ids * TOPK - jnp.minimum(row_ids, hot_rows)
    offset = jnp.where(has_hot[:, None], col_ids[None, :] - 1, col_ids[None, :])
    cold_index = jnp.maximum(start[:, None] + offset, 0)
    first_col = has_hot[:, None] & (col_ids[None, :] == 0)
    hot_pick = hot_set[row_ids % HOT]

    def one_device(device):
        cycle = jax.random.permutation(jax.random.fold_in(cold_key, device), cold_count).astype(jnp.int32)
        cold_picks = cold_set[cycle[cold_index % cold_count]]
        chosen = jnp.where(first_col, hot_pick[:, None], cold_picks)
        row_order = jax.random.permutation(jax.random.fold_in(row_key, device), TOK_DEV).astype(jnp.int32)
        shuffled = chosen[row_order]
        sub_keys = jax.random.split(jax.random.fold_in(col_key, device), TOK_DEV)
        columns = jax.vmap(lambda subkey: jax.random.permutation(subkey, TOPK))(sub_keys).astype(jnp.int32)
        return jnp.take_along_axis(shuffled, columns, axis=1)
    return jax.vmap(one_device)(jnp.arange(blocks, dtype=jnp.int32)).reshape(TOKENS, TOPK).astype(jnp.int32)


def levels(own_key, dims, shards, least, top_value):
    def one(axis_at, shards_of):
        steps = jax.random.uniform(jax.random.fold_in(jax.random.fold_in(own_key, 6), axis_at), (shards_of,), jnp.float32, least / len(shards), top_value / len(shards))
        return jnp.repeat(jnp.exp(steps), dims[axis_at] // shards_of).reshape((-1,) + (1,) * (len(dims) - axis_at - 1))

    loudness = one(*shards[0])
    for cut in shards[1:]:
        loudness = loudness * one(*cut)
    return loudness


def normal_values(key, shape, scale, bound, pieces=(), kind=jnp.bfloat16):
    entries = jax.random.normal(key, shape, jnp.float32) * scale
    if len(pieces) > 0:
        entries = levels(key, shape, pieces, -0.22, 0.18) * entries
    return jnp.clip(entries, min=-bound, max=bound).astype(kind)


def setup_inputs(seed: int = 0) -> dict:
    key_list = jax.random.split(jax.random.key(seed), 8)
    tokens = normal_values(key_list[0], (TOKENS, D), 1.0, 6.0, ((0, 128),))
    cotangent = normal_values(key_list[1], (TOKENS, D), 1.0, 6.0, ((0, 128),))
    routing = draw_routing(jax.random.fold_in(key_list[7], 71), 0)
    combine_weights = jnp.clip(0.05 + 0.25 * jax.random.uniform(key_list[3], (TOKENS, TOPK), jnp.float32) ** levels(key_list[3], (TOKENS, TOPK), ((0, 128),), -0.2, 0.2), 0.05, 0.3)
    w_gate = normal_values(key_list[4], (EXPERTS, D, HID), D ** -0.5, 0.09375, ((0, 64), (2, 2)))
    w_up = normal_values(key_list[5], (EXPERTS, D, HID), D ** -0.5, 0.09375, ((0, 64), (2, 2)))
    w_down = normal_values(key_list[6], (EXPERTS, HID, D), HID ** -0.5, 0.21875, ((0, 64), (1, 2)))
    return dict(tokens=tokens, cotangent=cotangent, routing=routing, combine_weights=combine_weights, w_gate=w_gate, w_up=w_up, w_down=w_down)


def silu_parts(gate_pre):
    sig_gate = jax.nn.sigmoid(gate_pre)
    return gate_pre * sig_gate, sig_gate


def expert_pass(row_tokens, route_grad, gate_matrix, up_matrix, down_matrix):
    gate_pre = jnp.dot(row_tokens, gate_matrix, preferred_element_type=jnp.float32)
    up_pre = jnp.dot(row_tokens, up_matrix, preferred_element_type=jnp.float32)
    activated, sig_gate = silu_parts(gate_pre)
    hidden = (activated * up_pre).astype(jnp.bfloat16)
    expert_out = jnp.dot(hidden, down_matrix, preferred_element_type=jnp.float32)
    hidden_grad = jnp.dot(route_grad, down_matrix.T, preferred_element_type=jnp.float32)
    up_grad = (hidden_grad * activated).astype(jnp.bfloat16)
    gate_grad = (hidden_grad * up_pre * sig_gate * (1.0 + gate_pre * (1.0 - sig_gate))).astype(jnp.bfloat16)
    input_grad = jnp.dot(gate_grad, gate_matrix.T, preferred_element_type=jnp.float32) + jnp.dot(up_grad, up_matrix.T, preferred_element_type=jnp.float32)
    gate_wgrad = jnp.dot(row_tokens.T, gate_grad, preferred_element_type=jnp.float32)
    up_wgrad = jnp.dot(row_tokens.T, up_grad, preferred_element_type=jnp.float32)
    down_wgrad = jnp.dot(hidden.T, route_grad, preferred_element_type=jnp.float32)
    return expert_out, input_grad, gate_wgrad, up_wgrad, down_wgrad


def reference(tokens, cotangent, routing, combine_weights, w_gate, w_up, w_down):
    count_all = TOKENS * TOPK
    flat_experts = routing.reshape(-1).astype(jnp.int32)
    flat_weights = combine_weights.reshape(-1)
    sorted_ids = jnp.argsort(flat_experts, stable=True).astype(jnp.int32)
    expert_ids = jnp.arange(EXPERTS, dtype=jnp.int32)
    counts = jnp.sum((flat_experts[:, None] == expert_ids[None, :]).astype(jnp.int32), axis=0)
    starts = (jnp.cumsum(counts) - counts).astype(jnp.int32)
    ranking = jnp.argsort(-(counts * EXPERTS + (EXPERTS - 1 - expert_ids)), stable=True).astype(jnp.int32)
    blocks = TOKENS // TOK_DEV

    def make_step(span_rows):
        def expert_step(totals, expert):
            combined, token_grad = totals
            lane_ids = jnp.arange(span_rows, dtype=jnp.int32)
            is_valid = lane_ids < counts[expert]
            assign = sorted_ids[jnp.clip(starts[expert] + lane_ids, 0, count_all - 1)]
            token_ids = (assign // TOPK).astype(jnp.int32)
            weight = jnp.where(is_valid, flat_weights[assign], 0.0).astype(jnp.float32)
            row_tokens = jnp.where(is_valid[:, None], tokens[token_ids], jnp.zeros((), jnp.bfloat16))
            route_grad = (weight[:, None] * cotangent[token_ids].astype(jnp.float32)).astype(jnp.bfloat16)
            expert_out, input_grad, gate_wgrad, up_wgrad, down_wgrad = expert_pass(
                row_tokens, route_grad, w_gate[expert], w_up[expert], w_down[expert])
            out_round = lax.optimization_barrier(expert_out.astype(jnp.bfloat16)).astype(jnp.float32)
            grad_round = lax.optimization_barrier(input_grad.astype(jnp.bfloat16)).astype(jnp.float32)
            combined = combined.at[token_ids].add(weight[:, None] * out_round)
            token_grad = token_grad.at[token_ids].add(jnp.where(is_valid[:, None], grad_round, 0.0))
            return (combined, token_grad), (gate_wgrad.astype(jnp.bfloat16), up_wgrad.astype(jnp.bfloat16), down_wgrad.astype(jnp.bfloat16))
        return expert_step

    zero_init = (jnp.zeros((TOKENS, D), jnp.float32), jnp.zeros((TOKENS, D), jnp.float32))
    totals, hot_grads = lax.scan(make_step(CAP * blocks), zero_init, ranking[:HOT])
    totals, cold_grads = lax.scan(make_step(CAP_COLD * blocks), totals, ranking[HOT:])
    inverse = jnp.argsort(ranking).astype(jnp.int32)
    grads = [jnp.take(jnp.concatenate([hot_part, cold_part], axis=0), inverse, axis=0)
             for hot_part, cold_part in zip(hot_grads, cold_grads)]
    return totals[0].astype(jnp.bfloat16), totals[1].astype(jnp.bfloat16), grads[0], grads[1], grads[2]
```

```python
import jax
import jax.numpy as jnp
from jax import lax
from jax.experimental import pallas as pl
from jax.experimental.pallas import tpu as pltpu
from jax.sharding import PartitionSpec as P

HOT = 4
BLOCK = 256
BF16 = jnp.bfloat16
F32 = jnp.float32


def dot(left, right, dims):
    return lax.dot_general(left, right, (dims, ((), ())), preferred_element_type=F32)


def swap(value):
    return lax.ppermute(value, "dp", [(0, 1), (1, 0)])


def exchange(value, experts):
    rows, features = value.shape
    parts = value.reshape(experts, rows // experts, features)
    moved = lax.all_to_all(parts, "expert", split_axis=0, concat_axis=0, tiled=True)
    return moved.reshape(rows, features)


def hidden_parts(rows, gate_matrix, up_matrix):
    gate_pre = dot(rows, gate_matrix, ((1,), (0,)))
    up_pre = dot(rows, up_matrix, ((1,), (0,)))
    sig_gate = jax.nn.sigmoid(gate_pre)
    activated = gate_pre * sig_gate
    hidden = (activated * up_pre).astype(BF16)
    gate_slope = up_pre * sig_gate * (1.0 + gate_pre * (1.0 - sig_gate))
    return hidden, activated, gate_slope


def hidden_kernel(rows_ref, gate_ref, up_ref, hidden_ref, act_ref, slope_ref):
    hidden_ref[...], act_ref[...], slope_ref[...] = hidden_parts(rows_ref[...], gate_ref[...], up_ref[...])


def forward_kernel(rows_ref, gate_ref, up_ref, down_ref, hidden_ref, act_ref, slope_ref, out_ref):
    hidden, act_ref[...], slope_ref[...] = hidden_parts(rows_ref[...], gate_ref[...], up_ref[...])
    hidden_ref[...] = hidden
    out_ref[...] = dot(hidden, down_ref[...], ((1,), (0,))).astype(BF16)


def out_kernel(hidden_ref, peer_ref, down_ref, out_ref):
    total = dot(hidden_ref[...], down_ref[...], ((1,), (0,))) + peer_ref[...].astype(F32)
    out_ref[...] = total.astype(BF16)


def grad_parts(grads, act, slope, down_matrix):
    hidden_grad = dot(grads, down_matrix, ((1,), (1,)))
    return (hidden_grad * slope).astype(BF16), (hidden_grad * act).astype(BF16)


def input_parts(gate_grad, up_grad, gate_matrix, up_matrix):
    return dot(gate_grad, gate_matrix, ((1,), (1,))) + dot(up_grad, up_matrix, ((1,), (1,)))


def grad_kernel(grads_ref, act_ref, slope_ref, down_ref, gate_grad_ref, up_grad_ref):
    gate_grad_ref[...], up_grad_ref[...] = grad_parts(grads_ref[...], act_ref[...], slope_ref[...], down_ref[...])


def backward_kernel(grads_ref, act_ref, slope_ref, gate_ref, up_ref, down_ref, gate_grad_ref, up_grad_ref, input_ref):
    gate_grad, up_grad = grad_parts(grads_ref[...], act_ref[...], slope_ref[...], down_ref[...])
    gate_grad_ref[...] = gate_grad
    up_grad_ref[...] = up_grad
    input_ref[...] = input_parts(gate_grad, up_grad, gate_ref[...], up_ref[...]).astype(BF16)


def input_kernel(gate_grad_ref, up_grad_ref, peer_ref, gate_ref, up_ref, input_ref):
    total = input_parts(gate_grad_ref[...], up_grad_ref[...], gate_ref[...], up_ref[...])
    input_ref[...] = (total + peer_ref[...].astype(F32)).astype(BF16)


def by_rows(kernel, row_args, matrices, outs):
    rows = row_args[0].shape[0]
    in_specs = [pl.BlockSpec((BLOCK, arg.shape[1]), lambda i: (i, 0)) for arg in row_args]
    in_specs += [
        pl.BlockSpec(matrix.shape, lambda i: (0, 0), pipeline_mode=pl.Buffered(1)) for matrix in matrices
    ]
    return pl.pallas_call(
        kernel,
        grid=(rows // BLOCK,),
        in_specs=in_specs,
        out_specs=[pl.BlockSpec((BLOCK, columns), lambda i: (i, 0)) for columns, _ in outs],
        out_shape=[jax.ShapeDtypeStruct((rows, columns), kind) for columns, kind in outs],
        compiler_params=pltpu.CompilerParams(vmem_limit_bytes=48 * 1024 * 1024),
        cost_estimate=pl.CostEstimate(flops=1000, bytes_accessed=1000, transcendentals=0),
    )(*row_args, *matrices)


def local(tokens, cotangent, routing, combine_weights, w_gate, w_up, w_down):
    tok_rows, features = tokens.shape
    top_count = routing.shape[1]
    experts = lax.axis_size("expert")
    cold_count = experts - HOT
    hot_cap = 2 * tok_rows * top_count // experts
    cold_cap = (tok_rows * top_count - HOT * hot_cap + cold_count - 1) // cold_count
    capacity = max(hot_cap, cold_cap)
    local_rows = experts * capacity
    gate_matrix, up_matrix, down_matrix = w_gate[0], w_up[0], w_down[0]
    width = gate_matrix.shape[1]

    flat_ids = routing.reshape(-1)
    expert_ids = jnp.arange(experts, dtype=jnp.int32)
    matches = (flat_ids[:, None] == expert_ids[None, :]).astype(jnp.int32)
    before = jnp.cumsum(matches, axis=0) - matches
    slot_ids = jnp.sum(before * matches, axis=1)
    position = (flat_ids * capacity + slot_ids).reshape(tok_rows, top_count)
    targets = jnp.arange(local_rows, dtype=jnp.int32)
    selected = position[None, :, :] == targets[:, None, None]
    picker = jnp.any(selected, axis=2).astype(BF16)
    slot_weight = jnp.sum(jnp.where(selected, combine_weights[None, :, :], 0.0), axis=(1, 2))

    send_rows = dot(picker, tokens, ((1,), (0,))).astype(BF16)
    rows_own = exchange(send_rows, experts)
    send_grads = (slot_weight[:, None] * dot(picker, cotangent, ((1,), (0,)))).astype(BF16)
    rows_own, send_grads = lax.optimization_barrier((rows_own, send_grads))
    grads_own = exchange(send_grads, experts)

    kept = [(width, BF16), (width, F32), (width, F32)]
    rows_other = swap(rows_own)
    hidden_own, act_own, slope_own = by_rows(hidden_kernel, [rows_own], [gate_matrix, up_matrix], kept)
    hidden_other, act_other, slope_other, out_other = by_rows(
        forward_kernel, [rows_other], [gate_matrix, up_matrix, down_matrix], kept + [(features, BF16)]
    )
    out_peer = swap(out_other)
    (out_send,) = by_rows(out_kernel, [hidden_own, out_peer], [down_matrix], [(features, BF16)])
    grads_own, out_send = lax.optimization_barrier((grads_own, out_send))
    out_back = exchange(out_send, experts)

    pair = [(width, BF16), (width, BF16)]
    grads_other = swap(grads_own)
    gate_own, up_own = by_rows(grad_kernel, [grads_own, act_own, slope_own], [down_matrix], pair)
    gate_other, up_other, input_other = by_rows(
        backward_kernel,
        [grads_other, act_other, slope_other],
        [gate_matrix, up_matrix, down_matrix],
        pair + [(features, BF16)],
    )
    input_peer = swap(input_other)
    (input_send,) = by_rows(
        input_kernel, [gate_own, up_own, input_peer], [gate_matrix, up_matrix], [(features, BF16)]
    )
    out_back, input_send = lax.optimization_barrier((out_back, input_send))
    input_back = exchange(input_send, experts)

    rows_all = jnp.concatenate([rows_own, rows_other])
    grads_all = jnp.concatenate([grads_own, grads_other])
    gate_wgrad = dot(rows_all, jnp.concatenate([gate_own, gate_other]), ((0,), (0,)))
    up_wgrad = dot(rows_all, jnp.concatenate([up_own, up_other]), ((0,), (0,)))
    down_wgrad = dot(jnp.concatenate([hidden_own, hidden_other]), grads_all, ((0,), (0,)))

    combined = jnp.zeros((tok_rows, features), F32)
    for column in range(top_count):
        column_pick = (position[:, column][:, None] == targets[None, :]).astype(BF16)
        column_rows = dot(column_pick, out_back, ((1,), (0,)))
        combined = combined + combine_weights[:, column][:, None] * column_rows
    gate_wgrad, up_wgrad, down_wgrad, combined, input_back = lax.optimization_barrier(
        (gate_wgrad.astype(BF16), up_wgrad.astype(BF16), down_wgrad.astype(BF16), combined.astype(BF16), input_back)
    )
    token_grad = dot(picker, input_back, ((0,), (0,))).astype(BF16)
    return combined, token_grad, gate_wgrad[None], up_wgrad[None], down_wgrad[None]


def solution(mesh):
    in_specs = (
        P(("dp", "expert"), None),
        P(("dp", "expert"), None),
        P(("dp", "expert"), None),
        P(("dp", "expert"), None),
        P("expert", None, "dp"),
        P("expert", None, "dp"),
        P("expert", "dp", None),
    )
    out_specs = (
        P(("dp", "expert"), None),
        P(("dp", "expert"), None),
        P("expert", None, "dp"),
        P("expert", None, "dp"),
        P("expert", "dp", None),
    )
    return jax.shard_map(local, mesh=mesh, in_specs=in_specs, out_specs=out_specs, check_vma=False)
```

```python
import jax
import jax.numpy as jnp
from jax import lax
from jax.experimental import pallas as pl
from jax.experimental.pallas import tpu as pltpu
from jax.sharding import PartitionSpec as P

HOT = 4
BLOCK = 256
BF16 = jnp.bfloat16
F32 = jnp.float32


def dot(left, right, dims):
    return lax.dot_general(left, right, (dims, ((), ())), preferred_element_type=F32)


def swap(value):
    size = value.shape[0] // 4
    parts = [value[size * i : size * (i + 1)] for i in range(4)]
    return jnp.concatenate([lax.ppermute(part, "dp", [(0, 1), (1, 0)]) for part in parts])


def exchange(value, experts):
    rows, features = value.shape
    parts = value.reshape(experts, rows // experts, features)
    moved = lax.all_to_all(parts, "expert", split_axis=0, concat_axis=0, tiled=True)
    return moved.reshape(rows, features)


def hidden_parts(rows, gate_matrix, up_matrix):
    gate_pre = dot(rows, gate_matrix, ((1,), (0,)))
    up_pre = dot(rows, up_matrix, ((1,), (0,)))
    sig_gate = jax.nn.sigmoid(gate_pre)
    activated = gate_pre * sig_gate
    hidden = (activated * up_pre).astype(BF16)
    gate_slope = up_pre * sig_gate * (1.0 + gate_pre * (1.0 - sig_gate))
    return hidden, activated, gate_slope


def hidden_kernel(rows_ref, gate_ref, up_ref, hidden_ref, act_ref, slope_ref):
    hidden_ref[...], act_ref[...], slope_ref[...] = hidden_parts(rows_ref[...], gate_ref[...], up_ref[...])


def forward_kernel(rows_ref, gate_ref, up_ref, down_ref, hidden_ref, act_ref, slope_ref, out_ref):
    hidden, act_ref[...], slope_ref[...] = hidden_parts(rows_ref[...], gate_ref[...], up_ref[...])
    hidden_ref[...] = hidden
    out_ref[...] = dot(hidden, down_ref[...], ((1,), (0,))).astype(BF16)


def out_kernel(hidden_ref, peer_ref, down_ref, out_ref):
    total = dot(hidden_ref[...], down_ref[...], ((1,), (0,))) + peer_ref[...].astype(F32)
    out_ref[...] = total.astype(BF16)


def grad_parts(grads, act, slope, down_matrix):
    hidden_grad = dot(grads, down_matrix, ((1,), (1,)))
    return (hidden_grad * slope).astype(BF16), (hidden_grad * act).astype(BF16)


def input_parts(gate_grad, up_grad, gate_matrix, up_matrix):
    return dot(gate_grad, gate_matrix, ((1,), (1,))) + dot(up_grad, up_matrix, ((1,), (1,)))


def grad_kernel(grads_ref, act_ref, slope_ref, down_ref, gate_grad_ref, up_grad_ref):
    gate_grad_ref[...], up_grad_ref[...] = grad_parts(grads_ref[...], act_ref[...], slope_ref[...], down_ref[...])


def backward_kernel(grads_ref, act_ref, slope_ref, gate_ref, up_ref, down_ref, gate_grad_ref, up_grad_ref, input_ref):
    gate_grad, up_grad = grad_parts(grads_ref[...], act_ref[...], slope_ref[...], down_ref[...])
    gate_grad_ref[...] = gate_grad
    up_grad_ref[...] = up_grad
    input_ref[...] = input_parts(gate_grad, up_grad, gate_ref[...], up_ref[...]).astype(BF16)


def input_kernel(gate_grad_ref, up_grad_ref, peer_ref, gate_ref, up_ref, input_ref):
    total = input_parts(gate_grad_ref[...], up_grad_ref[...], gate_ref[...], up_ref[...])
    input_ref[...] = (total + peer_ref[...].astype(F32)).astype(BF16)


def by_rows(kernel, row_args, matrices, outs):
    rows = row_args[0].shape[0]
    in_specs = [pl.BlockSpec((BLOCK, arg.shape[1]), lambda i: (i, 0)) for arg in row_args]
    in_specs += [
        pl.BlockSpec(matrix.shape, lambda i: (0, 0), pipeline_mode=pl.Buffered(1)) for matrix in matrices
    ]
    return pl.pallas_call(
        kernel,
        grid=(rows // BLOCK,),
        in_specs=in_specs,
        out_specs=[pl.BlockSpec((BLOCK, columns), lambda i: (i, 0)) for columns, _ in outs],
        out_shape=[jax.ShapeDtypeStruct((rows, columns), kind) for columns, kind in outs],
        compiler_params=pltpu.CompilerParams(vmem_limit_bytes=48 * 1024 * 1024),
        cost_estimate=pl.CostEstimate(flops=1000, bytes_accessed=1000, transcendentals=0),
    )(*row_args, *matrices)


def local(tokens, cotangent, routing, combine_weights, w_gate, w_up, w_down):
    tok_rows, features = tokens.shape
    top_count = routing.shape[1]
    experts = lax.axis_size("expert")
    cold_count = experts - HOT
    hot_cap = 2 * tok_rows * top_count // experts
    cold_cap = (tok_rows * top_count - HOT * hot_cap + cold_count - 1) // cold_count
    capacity = max(hot_cap, cold_cap)
    local_rows = experts * capacity
    gate_matrix, up_matrix, down_matrix = w_gate[0], w_up[0], w_down[0]
    width = gate_matrix.shape[1]

    flat_ids = routing.reshape(-1)
    expert_ids = jnp.arange(experts, dtype=jnp.int32)
    matches = (flat_ids[:, None] == expert_ids[None, :]).astype(jnp.int32)
    before = jnp.cumsum(matches, axis=0) - matches
    slot_ids = jnp.sum(before * matches, axis=1)
    position = (flat_ids * capacity + slot_ids).reshape(tok_rows, top_count)
    targets = jnp.arange(local_rows, dtype=jnp.int32)
    selected = position[None, :, :] == targets[:, None, None]
    picker = jnp.any(selected, axis=2).astype(BF16)
    slot_weight = jnp.sum(jnp.where(selected, combine_weights[None, :, :], 0.0), axis=(1, 2))

    send_rows = dot(picker, tokens, ((1,), (0,))).astype(BF16)
    rows_own = exchange(send_rows, experts)
    send_grads = (slot_weight[:, None] * dot(picker, cotangent, ((1,), (0,)))).astype(BF16)
    rows_own, send_grads = lax.optimization_barrier((rows_own, send_grads))
    grads_own = exchange(send_grads, experts)

    kept = [(width, BF16), (width, F32), (width, F32)]
    rows_other = swap(rows_own)
    hidden_own, act_own, slope_own = by_rows(hidden_kernel, [rows_own], [gate_matrix, up_matrix], kept)
    hidden_other, act_other, slope_other, out_other = by_rows(
        forward_kernel, [rows_other], [gate_matrix, up_matrix, down_matrix], kept + [(features, BF16)]
    )
    out_peer = swap(out_other)
    (out_send,) = by_rows(out_kernel, [hidden_own, out_peer], [down_matrix], [(features, BF16)])
    grads_own, out_send = lax.optimization_barrier((grads_own, out_send))
    out_back = exchange(out_send, experts)

    pair = [(width, BF16), (width, BF16)]
    grads_other = swap(grads_own)
    gate_own, up_own = by_rows(grad_kernel, [grads_own, act_own, slope_own], [down_matrix], pair)
    gate_other, up_other, input_other = by_rows(
        backward_kernel,
        [grads_other, act_other, slope_other],
        [gate_matrix, up_matrix, down_matrix],
        pair + [(features, BF16)],
    )
    input_peer = swap(input_other)
    (input_send,) = by_rows(
        input_kernel, [gate_own, up_own, input_peer], [gate_matrix, up_matrix], [(features, BF16)]
    )
    out_back, input_send = lax.optimization_barrier((out_back, input_send))
    input_back = exchange(input_send, experts)

    rows_all = jnp.concatenate([rows_own, rows_other])
    grads_all = jnp.concatenate([grads_own, grads_other])
    gate_wgrad = dot(rows_all, jnp.concatenate([gate_own, gate_other]), ((0,), (0,)))
    up_wgrad = dot(rows_all, jnp.concatenate([up_own, up_other]), ((0,), (0,)))
    down_wgrad = dot(jnp.concatenate([hidden_own, hidden_other]), grads_all, ((0,), (0,)))

    combined = jnp.zeros((tok_rows, features), F32)
    for column in range(top_count):
        column_pick = (position[:, column][:, None] == targets[None, :]).astype(BF16)
        column_rows = dot(column_pick, out_back, ((1,), (0,)))
        combined = combined + combine_weights[:, column][:, None] * column_rows
    gate_wgrad, up_wgrad, down_wgrad, combined, input_back = lax.optimization_barrier(
        (gate_wgrad.astype(BF16), up_wgrad.astype(BF16), down_wgrad.astype(BF16), combined.astype(BF16), input_back)
    )
    token_grad = dot(picker, input_back, ((0,), (0,))).astype(BF16)
    return combined, token_grad, gate_wgrad[None], up_wgrad[None], down_wgrad[None]


def solution(mesh):
    in_specs = (
        P(("dp", "expert"), None),
        P(("dp", "expert"), None),
        P(("dp", "expert"), None),
        P(("dp", "expert"), None),
        P("expert", None, "dp"),
        P("expert", None, "dp"),
        P("expert", "dp", None),
    )
    out_specs = (
        P(("dp", "expert"), None),
        P(("dp", "expert"), None),
        P("expert", None, "dp"),
        P("expert", None, "dp"),
        P("expert", "dp", None),
    )
    return jax.shard_map(local, mesh=mesh, in_specs=in_specs, out_specs=out_specs, check_vma=False)
```

```python
import jax
import jax.numpy as jnp
from jax import lax
from jax.experimental import pallas as pl
from jax.experimental.pallas import tpu as pltpu
from jax.sharding import PartitionSpec as P

HOT = 4
SIDE = 4
COLUMNS = 512
BF16 = jnp.bfloat16
F32 = jnp.float32
MIB = 1024 * 1024


def dot(left, right, dims):
    return lax.dot_general(left, right, (dims, ((), ())), preferred_element_type=F32)


def swap(value):
    return lax.ppermute(value, "dp", [(0, 1), (1, 0)])


def swap_halves(value):
    half = value.shape[0] // 2
    return [swap(value[:half]), swap(value[half:])]


def shift(value, axis, steps):
    pairs = []
    for chip in range(SIDE**3):
        place = [chip // SIDE**2, chip // SIDE % SIDE, chip % SIDE]
        place[axis] = (place[axis] + steps) % SIDE
        pairs.append((chip, (place[0] * SIDE + place[1]) * SIDE + place[2]))
    return lax.ppermute(value, "expert", pairs)


def exchange(value, experts):
    rows, features = value.shape
    parts = value.reshape(experts, rows // experts, features)
    moved = lax.all_to_all(parts, "expert", split_axis=0, concat_axis=0, tiled=True)
    return moved.reshape(rows, features)


def call(kernel, args, outs, limit, grid=None):
    in_specs = [spec for _, spec in args]
    return pl.pallas_call(
        kernel,
        grid=grid or (),
        in_specs=in_specs,
        out_specs=[spec for _, _, spec in outs],
        out_shape=[jax.ShapeDtypeStruct(shape, kind) for shape, kind, _ in outs],
        compiler_params=pltpu.CompilerParams(vmem_limit_bytes=limit * MIB),
        cost_estimate=pl.CostEstimate(flops=1000, bytes_accessed=1000, transcendentals=0),
    )(*[arg for arg, _ in args])


def whole(arg):
    return arg, pl.BlockSpec(memory_space=pltpu.VMEM)


def out_whole(shape, kind):
    return shape, kind, pl.BlockSpec(memory_space=pltpu.VMEM)


def joined(refs, part=None):
    if part is None:
        return jnp.concatenate([ref[...] for ref in refs], axis=0)
    half = refs[0].shape[0] // 2
    return jnp.concatenate([ref[part * half : (part + 1) * half] for ref in refs], axis=0)


def hidden_parts(rows, gate_matrix, up_matrix):
    gate_pre = dot(rows, gate_matrix, ((1,), (0,)))
    up_pre = dot(rows, up_matrix, ((1,), (0,)))
    sig_gate = jax.nn.sigmoid(gate_pre)
    activated = gate_pre * sig_gate
    hidden = (activated * up_pre).astype(BF16)
    gate_slope = up_pre * sig_gate * (1.0 + gate_pre * (1.0 - sig_gate))
    return hidden, activated, gate_slope


def grad_parts(grads, act, slope, down_matrix):
    hidden_grad = dot(grads, down_matrix, ((1,), (1,)))
    return (hidden_grad * slope).astype(BF16), (hidden_grad * act).astype(BF16)


def input_parts(gate_grad, up_grad, gate_matrix, up_matrix):
    return dot(gate_grad, gate_matrix, ((1,), (1,))) + dot(up_grad, up_matrix, ((1,), (1,)))


def forward_kernel(own_ref, peer0_ref, peer1_ref, gate_ref, up_ref, down_ref, hidden_ref, act_ref, slope_ref, out0_ref, out1_ref):
    rows = joined([own_ref, peer0_ref, peer1_ref])
    hidden, act_ref[...], slope_ref[...] = hidden_parts(rows, gate_ref[...], up_ref[...])
    hidden_ref[...] = hidden
    own = own_ref.shape[0]
    half = own // 2
    out0_ref[...] = dot(hidden[own : own + half], down_ref[...], ((1,), (0,))).astype(BF16)
    out1_ref[...] = dot(hidden[own + half :], down_ref[...], ((1,), (0,))).astype(BF16)


def out_kernel(hidden_ref, peer0_ref, peer1_ref, down_ref, out_ref):
    own = out_ref.shape[0]
    total = dot(hidden_ref[:own], down_ref[...], ((1,), (0,))) + joined([peer0_ref, peer1_ref]).astype(F32)
    out_ref[...] = total.astype(BF16)


def backward_kernel(own_ref, peer0_ref, peer1_ref, act_ref, slope_ref, gate_ref, up_ref, down_ref, gate_grad_ref, up_grad_ref, in0_ref, in1_ref):
    grads = joined([own_ref, peer0_ref, peer1_ref])
    gate_grad, up_grad = grad_parts(grads, act_ref[...], slope_ref[...], down_ref[...])
    gate_grad_ref[...] = gate_grad
    up_grad_ref[...] = up_grad
    own = own_ref.shape[0]
    half = own // 2
    for start, in_ref in ((own, in0_ref), (own + half, in1_ref)):
        rows = slice(start, start + half)
        in_ref[...] = input_parts(gate_grad[rows], up_grad[rows], gate_ref[...], up_ref[...]).astype(BF16)


def input_kernel(gate_grad_ref, up_grad_ref, peer0_ref, peer1_ref, gate_ref, up_ref, out_ref):
    own = out_ref.shape[0]
    total = input_parts(gate_grad_ref[:own], up_grad_ref[:own], gate_ref[...], up_ref[...])
    out_ref[...] = (total + joined([peer0_ref, peer1_ref]).astype(F32)).astype(BF16)


def extra_kernel(*refs):
    blocks, (gate_ref, up_ref, down_ref, hidden_ref, gate_grad_ref, up_grad_ref) = refs[:8], refs[8:14]
    sends = refs[14:]
    hidden, act, slope = hidden_parts(joined(blocks, 0), gate_ref[...], up_ref[...])
    gate_grad, up_grad = grad_parts(joined(blocks, 1), act, slope, down_ref[...])
    hidden_ref[...], gate_grad_ref[...], up_grad_ref[...] = hidden, gate_grad, up_grad
    own = hidden.shape[0] // 2
    out = dot(hidden[own:], down_ref[...], ((1,), (0,))).astype(BF16)
    back = input_parts(gate_grad[own:], up_grad[own:], gate_ref[...], up_ref[...]).astype(BF16)
    half = sends[0].shape[0] // 2
    for i, send in enumerate(sends):
        send[:half] = out[i * half : (i + 1) * half]
        send[half:] = back[i * half : (i + 1) * half]


def extra_out_kernel(*refs):
    hidden_ref, gate_grad_ref, up_grad_ref, gate_ref, up_ref, down_ref = refs[:6]
    peers, sends = refs[6:10], refs[10:]
    own = hidden_ref.shape[0] // 2
    out = dot(hidden_ref[:own], down_ref[...], ((1,), (0,)))
    back = input_parts(gate_grad_ref[:own], up_grad_ref[:own], gate_ref[...], up_ref[...])
    half = sends[0].shape[0] // 2
    for i, (peer, send) in enumerate(zip(peers, sends)):
        send[:half] = (out[i * half : (i + 1) * half] + peer[:half].astype(F32)).astype(BF16)
        send[half:] = (back[i * half : (i + 1) * half] + peer[half:].astype(F32)).astype(BF16)


def choose_kernel(select_ref, *refs):
    pieces, outs = refs[:SIDE], refs[SIDE:]
    chosen = dot(select_ref[...], joined(pieces), ((1,), (0,))).astype(BF16)
    rows = outs[0].shape[0]
    for i, out in enumerate(outs):
        out[...] = chosen[i * rows : (i + 1) * rows]


def choose(select, pieces, out_rows):
    rows, features = pieces[0].shape
    column = lambda i: (0, i)
    args = [(select, pl.BlockSpec(select.shape, lambda i: (0, 0)))]
    args += [(piece, pl.BlockSpec((rows, COLUMNS), column)) for piece in pieces]
    outs = [((out_rows, features), BF16, pl.BlockSpec((out_rows, COLUMNS), column))] * SIDE
    return call(choose_kernel, args, outs, 32, grid=(features // COLUMNS,))


def weight_kernel(*refs):
    rows, grads = refs[:11], refs[11:22]
    hidden_m, hidden_e, gate_m, gate_e, up_m, up_e = refs[22:28]
    gate_out, up_out, down_out = refs[28:]
    all_rows = joined(rows)
    both = jnp.concatenate([joined([gate_m, gate_e]), joined([up_m, up_e])], axis=1)
    total = dot(all_rows, both, ((0,), (0,)))
    width = gate_out.shape[1]
    gate_out[...] = total[:, :width].astype(BF16)
    up_out[...] = total[:, width:].astype(BF16)
    down_out[...] = dot(joined([hidden_m, hidden_e]), joined(grads), ((0,), (0,))).astype(BF16)


def weight_grads(main_rows, main_grads, blocks, kept):
    features = main_rows[0].shape[1]
    width = kept[0].shape[1]
    half = blocks[0].shape[0] // 2
    column = lambda i: (0, i)
    args = []
    for part, mains in enumerate((main_rows, main_grads)):
        args += [(main, pl.BlockSpec((main.shape[0], COLUMNS), column)) for main in mains]
        args += [(block, pl.BlockSpec((half, COLUMNS), lambda i, part=part: (part, i))) for block in blocks]
    args += [(value, pl.BlockSpec(value.shape, lambda i: (0, 0))) for value in kept]
    tall = ((features, width), BF16, pl.BlockSpec((COLUMNS, width), lambda i: (i, 0)))
    wide = ((width, features), BF16, pl.BlockSpec((width, COLUMNS), column))
    return call(weight_kernel, args, [tall, tall, wide], 40, grid=(features // COLUMNS,))


def combine_kernel(position_ref, weight_ref, main_ref, *refs):
    extras, out_ref = refs[:SIDE], refs[SIDE]
    main = main_ref[...]
    extra = sum(ref[...].astype(F32) for ref in extras).astype(BF16)
    tok_rows, top_count = position_ref.shape
    main_ids = lax.broadcasted_iota(jnp.int32, (tok_rows, main.shape[0]), 1)
    extra_ids = lax.broadcasted_iota(jnp.int32, (tok_rows, extra.shape[0]), 1) + main.shape[0]
    total = jnp.zeros(out_ref.shape, F32)
    for column in range(top_count):
        position = position_ref[:, column : column + 1]
        found = dot((position == main_ids).astype(F32).astype(BF16), main, ((1,), (0,)))
        found += dot((position == extra_ids).astype(F32).astype(BF16), extra, ((1,), (0,)))
        total += weight_ref[:, column : column + 1] * found
    out_ref[...] = total.astype(BF16)


def combine(position, weights, main, extras, part):
    rows, features = main.shape
    tok_rows = position.shape[0]
    wide = features // 4
    half = extras[0].shape[0] // 2
    fixed = lambda i: (0, 0)
    args = [(position, pl.BlockSpec(position.shape, fixed)), (weights, pl.BlockSpec(weights.shape, fixed))]
    args += [(main, pl.BlockSpec((rows, wide), lambda i: (0, i)))]
    args += [(extra, pl.BlockSpec((half, wide), lambda i: (part, i))) for extra in extras]
    outs = [((tok_rows, features), BF16, pl.BlockSpec((tok_rows, wide), lambda i: (0, i)))]
    return call(combine_kernel, args, outs, 24, grid=(4,))[0]


def digits(count, sizes):
    ids = jnp.arange(count, dtype=jnp.int32)
    found = []
    for size in reversed(sizes):
        found.append(ids % size)
        ids = ids // size
    return found[::-1]


def local(tokens, cotangent, routing, combine_weights, w_gate, w_up, w_down):
    tok_rows, features = tokens.shape
    top_count = routing.shape[1]
    experts = lax.axis_size("expert")
    cold_count = experts - HOT
    hot_cap = 2 * tok_rows * top_count // experts
    capacity = (tok_rows * top_count - HOT * hot_cap + cold_count - 1) // cold_count
    spare = hot_cap - capacity
    main_count = experts * capacity
    extra_count = HOT * spare
    gate_matrix, up_matrix, down_matrix = w_gate[0], w_up[0], w_down[0]
    width = gate_matrix.shape[1]

    flat_ids = routing.reshape(-1)
    expert_ids = jnp.arange(experts, dtype=jnp.int32)
    matches = (flat_ids[:, None] == expert_ids[None, :]).astype(jnp.int32)
    before = jnp.cumsum(matches, axis=0) - matches
    slot_ids = jnp.sum(before * matches, axis=1)
    is_hot = (jnp.sum(matches, axis=0) > capacity).astype(jnp.int32)
    hot_rank = jnp.sum(jnp.where(expert_ids[None, :] < expert_ids[:, None], is_hot[None, :], 0), axis=1)
    rank_ids = jnp.where(is_hot > 0, hot_rank, -1)
    route_rank = jnp.sum(matches * hot_rank[None, :], axis=1)
    main_position = flat_ids * capacity + slot_ids
    extra_position = main_count + route_rank * spare + slot_ids - capacity
    position = jnp.where(slot_ids < capacity, main_position, extra_position).reshape(tok_rows, top_count)
    targets = jnp.arange(main_count + extra_count, dtype=jnp.int32)
    selected = position[None, :, :] == targets[:, None, None]
    picker = jnp.any(selected, axis=2).astype(BF16)
    slot_weight = jnp.sum(jnp.where(selected, combine_weights[None, :, :], 0.0), axis=(1, 2))

    send_rows = dot(picker[:main_count], tokens, ((1,), (0,))).astype(BF16)
    rows_own = exchange(send_rows, experts)
    send_grads = (slot_weight[:main_count, None] * dot(picker[:main_count], cotangent, ((1,), (0,)))).astype(BF16)

    me = lax.axis_index("expert")
    here = [me // SIDE**2, me // SIDE % SIDE, me % SIDE]
    extra_rows = dot(picker[main_count:], tokens, ((1,), (0,))).astype(BF16)
    extra_grads = (slot_weight[main_count:, None] * dot(picker[main_count:], cotangent, ((1,), (0,)))).astype(BF16)
    along_x = jnp.concatenate([extra_rows, extra_grads])
    along_y = jnp.concatenate([along_x] + [shift(along_x, 2, step) for step in range(1, SIDE)])
    pieces = [along_y] + [shift(along_y, 1, step) for step in range(1, SIDE)]
    gathered = SIDE * SIDE * 2 * extra_count
    out_z, out_t, out_y, out_x, out_r = digits(gathered, (SIDE, 2, SIDE, SIDE, spare))
    in_y, in_x, in_t, in_h, in_r = digits(gathered, (SIDE, SIDE, 2, HOT, spare))
    steps = jnp.arange(SIDE, dtype=jnp.int32)
    line = ((here[0] + steps) % SIDE) * SIDE**2 + here[1] * SIDE + here[2]
    line_rank = jnp.sum(jnp.where(expert_ids[None, :] == line[:, None], rank_ids[None, :], 0), axis=1)
    out_rank = jnp.sum(jnp.where(out_z[:, None] == steps[None, :], line_rank[None, :], 0), axis=1)
    source = (out_y * SIDE + out_x) * 2 + out_t
    origin = (in_y * SIDE + in_x) * 2 + in_t
    to_line = (
        ((source * spare + out_r)[:, None] == (origin * spare + in_r)[None, :]) & (out_rank[:, None] == in_h[None, :])
    ).astype(BF16)
    blocks = choose(to_line, pieces, gathered // SIDE)
    blocks = [blocks[0]] + [shift(blocks[step], 0, step) for step in range(1, SIDE)]
    peer_blocks = [swap(block) for block in blocks]

    rows_own, send_grads = lax.optimization_barrier((rows_own, send_grads))
    grads_own = exchange(send_grads, experts)

    both = 2 * main_count
    half = (main_count // 2, features)
    rows_peer = swap_halves(rows_own)
    weights = [whole(matrix) for matrix in (gate_matrix, up_matrix, down_matrix)]
    hidden, act, slope, *outs = call(
        forward_kernel,
        [whole(value) for value in [rows_own] + rows_peer] + weights,
        [out_whole((both, width), kind) for kind in (BF16, F32, F32)] + [out_whole(half, BF16)] * 2,
        48,
    )
    outs = [swap(out) for out in outs]
    (out_send,) = call(
        out_kernel,
        [whole(value) for value in [hidden] + outs] + weights[2:],
        [out_whole((main_count, features), BF16)],
        32,
    )

    extra_both = 2 * SIDE**3 * spare
    block_shape = blocks[0].shape
    hidden_e, gate_e, up_e, *sends = call(
        extra_kernel,
        [whole(block) for block in blocks + peer_blocks] + weights,
        [out_whole((extra_both, width), BF16)] * 3 + [out_whole(block_shape, BF16)] * SIDE,
        56,
    )
    peers = [swap(send) for send in sends]
    backs = call(
        extra_out_kernel,
        [whole(value) for value in (hidden_e, gate_e, up_e)] + weights + [whole(peer) for peer in peers],
        [out_whole(block_shape, BF16)] * SIDE,
        48,
    )

    grads_own, out_send = lax.optimization_barrier((grads_own, out_send))
    out_back = exchange(out_send, experts)

    grads_peer = swap_halves(grads_own)
    gate_grad, up_grad, *ins = call(
        backward_kernel,
        [whole(value) for value in [grads_own] + grads_peer + [act, slope]] + weights,
        [out_whole((both, width), BF16)] * 2 + [out_whole(half, BF16)] * 2,
        48,
    )
    ins = [swap(value) for value in ins]
    (input_send,) = call(
        input_kernel,
        [whole(value) for value in [gate_grad, up_grad] + ins] + weights[:2],
        [out_whole((main_count, features), BF16)],
        32,
    )

    backs = [backs[0]] + [shift(backs[step], 0, -step) for step in range(1, SIDE)]
    group = SIDE * spare
    back_half = block_shape[0] // 2
    planes = []
    for step in range(SIDE):
        rows = [
            back[part * back_half + step * group : part * back_half + (step + 1) * group]
            for back in backs
            for part in range(2)
        ]
        plane = jnp.concatenate(rows)
        planes.append(plane if step == 0 else shift(plane, 1, -step))
    home_x, home_t, home_h, home_r = digits(SIDE * 2 * extra_count, (SIDE, 2, HOT, spare))
    in_y, in_z, in_t, in_x, in_r = digits(gathered, (SIDE, SIDE, 2, SIDE, spare))
    ranks = jnp.arange(HOT, dtype=jnp.int32)
    hot_ids = jnp.sum(jnp.where(rank_ids[None, :] == ranks[:, None], expert_ids[None, :], 0), axis=1)
    hot_step_y = (hot_ids // SIDE % SIDE - here[1]) % SIDE
    hot_step_z = (hot_ids // SIDE**2 - here[0]) % SIDE
    hot_here = jnp.where(hot_ids % SIDE == here[2], hot_step_y * SIDE + hot_step_z, -1)
    home_from = jnp.sum(jnp.where(home_h[:, None] == ranks[None, :], hot_here[None, :], 0), axis=1)
    to_home = (
        (((home_t * SIDE + home_x) * spare + home_r)[:, None] == ((in_t * SIDE + in_x) * spare + in_r)[None, :])
        & (home_from[:, None] == (in_y * SIDE + in_z)[None, :])
    ).astype(BF16)
    lasts = choose(to_home, planes, 2 * extra_count)
    lasts = [lasts[0]] + [shift(lasts[step], 2, -step) for step in range(1, SIDE)]

    out_back, input_send = lax.optimization_barrier((out_back, input_send))
    input_back = exchange(input_send, experts)

    wgrads = weight_grads(
        [rows_own] + rows_peer,
        [grads_own] + grads_peer,
        blocks + peer_blocks,
        [hidden, hidden_e, gate_grad, gate_e, up_grad, up_e],
    )
    combined = combine(position, combine_weights, out_back, lasts, 0)
    *wgrads, combined, input_back = lax.optimization_barrier((*wgrads, combined, input_back))
    token_grad = combine(position, jnp.ones_like(combine_weights), input_back, lasts, 1)
    return combined, token_grad, wgrads[0][None], wgrads[1][None], wgrads[2][None]


def solution(mesh):
    in_specs = (
        P(("dp", "expert"), None),
        P(("dp", "expert"), None),
        P(("dp", "expert"), None),
        P(("dp", "expert"), None),
        P("expert", None, "dp"),
        P("expert", None, "dp"),
        P("expert", "dp", None),
    )
    out_specs = (
        P(("dp", "expert"), None),
        P(("dp", "expert"), None),
        P("expert", None, "dp"),
        P("expert", None, "dp"),
        P("expert", "dp", None),
    )
    return jax.shard_map(local, mesh=mesh, in_specs=in_specs, out_specs=out_specs, check_vma=False)
```

```python
import functools

import jax
import jax.numpy as jnp
from jax import lax
from jax.experimental import pallas as pl
from jax.experimental.pallas import tpu as pltpu
from jax.sharding import PartitionSpec as P

HOT = 4
COLUMNS = 512
PARTS = 2
BF16 = jnp.bfloat16
F32 = jnp.float32
MIB = 1024 * 1024


def dot(left, right, dims):
    return lax.dot_general(left, right, (dims, ((), ())), preferred_element_type=F32)


def swap(value):
    return lax.ppermute(value, "dp", [(0, 1), (1, 0)])


def exchange(value, experts):
    rows, features = value.shape
    parts = value.reshape(experts, rows // experts, features)
    moved = lax.all_to_all(parts, "expert", split_axis=0, concat_axis=0, tiled=True)
    return moved.reshape(rows, features)


def call(kernel, args, outs, limit, grid=(), scratch=()):
    in_specs = [spec for _, spec in args]
    return pl.pallas_call(
        kernel,
        grid=grid,
        in_specs=in_specs,
        out_specs=[spec for _, _, spec in outs],
        out_shape=[jax.ShapeDtypeStruct(shape, kind) for shape, kind, _ in outs],
        scratch_shapes=scratch,
        compiler_params=pltpu.CompilerParams(vmem_limit_bytes=limit * MIB),
        cost_estimate=pl.CostEstimate(flops=1000, bytes_accessed=1000, transcendentals=0),
    )(*[arg for arg, _ in args])


def whole(arg):
    return arg, pl.BlockSpec(memory_space=pltpu.VMEM)


def fixed(arg):
    return arg, pl.BlockSpec(arg.shape, lambda i: (0, 0))


def across(arg):
    return arg, pl.BlockSpec((arg.shape[0], COLUMNS), lambda i: (0, i))


def out_whole(shape, kind):
    return shape, kind, pl.BlockSpec(memory_space=pltpu.VMEM)


def by_column(rows, columns, kind):
    return (rows, columns), kind, pl.BlockSpec((rows, COLUMNS), lambda i: (0, i))


def joined(refs):
    return jnp.concatenate([ref[...] for ref in refs], axis=0)


def hidden_parts(rows, gate_matrix, up_matrix):
    gate_pre = dot(rows, gate_matrix, ((1,), (0,)))
    up_pre = dot(rows, up_matrix, ((1,), (0,)))
    sig_gate = jax.nn.sigmoid(gate_pre)
    activated = gate_pre * sig_gate
    hidden = (activated * up_pre).astype(BF16)
    gate_slope = up_pre * sig_gate * (1.0 + gate_pre * (1.0 - sig_gate))
    return hidden, activated, gate_slope


def grad_parts(grads, act, slope, down_matrix):
    hidden_grad = dot(grads, down_matrix, ((1,), (1,)))
    return (hidden_grad * slope).astype(BF16), (hidden_grad * act).astype(BF16)


def input_parts(gate_grad, up_grad, gate_matrix, up_matrix):
    return dot(gate_grad, gate_matrix, ((1,), (1,))) + dot(up_grad, up_matrix, ((1,), (1,)))


def places(routing_ref, position_ref, experts, capacity):
    tok_rows, top_count = routing_ref.shape
    expert_ids = lax.broadcasted_iota(jnp.int32, (tok_rows, experts), 1)
    named = [routing_ref[:, column : column + 1] == expert_ids for column in range(top_count)]
    counts = sum(hit.astype(F32) for hit in named)
    earlier = lax.broadcasted_iota(jnp.int32, (tok_rows, tok_rows), 1) < lax.broadcasted_iota(
        jnp.int32, (tok_rows, tok_rows), 0
    )
    before = dot(earlier.astype(F32).astype(BF16), counts.astype(BF16), ((1,), (0,)))
    for column, hit in enumerate(named):
        slot = jnp.sum(jnp.where(hit, before, 0.0), axis=1, keepdims=True).astype(jnp.int32)
        position_ref[:, column : column + 1] = routing_ref[:, column : column + 1] * capacity + slot


def pick_matrix(position_ref, local_rows):
    tok_rows, top_count = position_ref.shape
    slots = lax.broadcasted_iota(jnp.int32, (tok_rows, local_rows), 1)
    return sum((position_ref[:, column : column + 1] == slots).astype(F32) for column in range(top_count)).astype(BF16)


def dispatch_kernel(routing_ref, tokens_ref, position_ref, out_ref, pick_ref, *, experts, capacity):
    @pl.when(pl.program_id(0) == 0)
    def _():
        places(routing_ref, position_ref, experts, capacity)
        pick_ref[...] = pick_matrix(position_ref, pick_ref.shape[1])

    out_ref[...] = dot(pick_ref[...], tokens_ref[...], ((0,), (0,))).astype(BF16)


def token_grad_kernel(position_ref, rows_ref, out_ref, pick_ref):
    @pl.when(pl.program_id(0) == 0)
    def _():
        pick_ref[...] = pick_matrix(position_ref, pick_ref.shape[1])

    out_ref[...] = dot(pick_ref[...], rows_ref[...], ((1,), (0,))).astype(BF16)


def combine_kernel(position_ref, weight_ref, rows_ref, out_ref):
    rows = rows_ref[...]
    tok_rows, top_count = position_ref.shape
    slots = lax.broadcasted_iota(jnp.int32, (tok_rows, rows.shape[0]), 1)
    total = jnp.zeros(out_ref.shape, F32)
    for column in range(top_count):
        pick = (position_ref[:, column : column + 1] == slots).astype(F32).astype(BF16)
        total += weight_ref[:, column : column + 1] * dot(pick, rows, ((1,), (0,)))
    out_ref[...] = total.astype(BF16)


def hidden_kernel(rows_ref, gate_ref, up_ref, hidden_ref, act_ref, slope_ref):
    hidden_ref[...], act_ref[...], slope_ref[...] = hidden_parts(rows_ref[...], gate_ref[...], up_ref[...])


def forward_kernel(rows_ref, gate_ref, up_ref, down_ref, hidden_ref, act_ref, slope_ref, *out_refs):
    hidden, act_ref[...], slope_ref[...] = hidden_parts(rows_ref[...], gate_ref[...], up_ref[...])
    hidden_ref[...] = hidden
    size = hidden.shape[0] // len(out_refs)
    for i, out_ref in enumerate(out_refs):
        out_ref[...] = dot(hidden[i * size : (i + 1) * size], down_ref[...], ((1,), (0,))).astype(BF16)


def out_kernel(hidden_ref, down_ref, *refs):
    peer_refs, out_ref = refs[:-1], refs[-1]
    size = hidden_ref.shape[0] // len(peer_refs)
    for i, peer_ref in enumerate(peer_refs):
        rows = slice(i * size, (i + 1) * size)
        total = dot(hidden_ref[rows], down_ref[...], ((1,), (0,))) + peer_ref[...].astype(F32)
        out_ref[rows] = total.astype(BF16)


def grad_kernel(grads_ref, act_ref, slope_ref, down_ref, gate_grad_ref, up_grad_ref):
    gate_grad_ref[...], up_grad_ref[...] = grad_parts(grads_ref[...], act_ref[...], slope_ref[...], down_ref[...])


def backward_kernel(grads_ref, act_ref, slope_ref, gate_ref, up_ref, down_ref, gate_grad_ref, up_grad_ref, *in_refs):
    gate_grad, up_grad = grad_parts(grads_ref[...], act_ref[...], slope_ref[...], down_ref[...])
    gate_grad_ref[...] = gate_grad
    up_grad_ref[...] = up_grad
    size = gate_grad.shape[0] // len(in_refs)
    for i, in_ref in enumerate(in_refs):
        rows = slice(i * size, (i + 1) * size)
        in_ref[...] = input_parts(gate_grad[rows], up_grad[rows], gate_ref[...], up_ref[...]).astype(BF16)


def input_kernel(gate_grad_ref, up_grad_ref, gate_ref, up_ref, *refs):
    peer_refs, out_ref = refs[:-1], refs[-1]
    size = gate_grad_ref.shape[0] // len(peer_refs)
    for i, peer_ref in enumerate(peer_refs):
        rows = slice(i * size, (i + 1) * size)
        total = input_parts(gate_grad_ref[rows], up_grad_ref[rows], gate_ref[...], up_ref[...])
        out_ref[rows] = (total + peer_ref[...].astype(F32)).astype(BF16)


def weight_kernel(*refs):
    rows, grads, hidden, gate_grad, up_grad = (refs[2 * i : 2 * i + 2] for i in range(5))
    gate_out, up_out, down_out = refs[10:]
    both = jnp.concatenate([joined(gate_grad), joined(up_grad)], axis=1)
    total = dot(joined(rows), both, ((0,), (0,)))
    width = gate_out.shape[1]
    gate_out[...] = total[:, :width].astype(BF16)
    up_out[...] = total[:, width:].astype(BF16)
    down_out[...] = dot(joined(hidden), joined(grads), ((0,), (0,))).astype(BF16)


def weight_grads(wide, kept):
    features = wide[0].shape[1]
    width = kept[0].shape[1]
    args = [(value, pl.BlockSpec((value.shape[0], COLUMNS), lambda i: (0, i))) for value in wide]
    args += [fixed(value) for value in kept]
    tall = ((features, width), BF16, pl.BlockSpec((COLUMNS, width), lambda i: (i, 0)))
    return call(weight_kernel, args, [tall, tall, by_column(width, features, BF16)], 48, grid=(features // COLUMNS,))


def local(tokens, cotangent, routing, combine_weights, w_gate, w_up, w_down):
    tok_rows, features = tokens.shape
    top_count = routing.shape[1]
    experts = lax.axis_size("expert")
    cold_count = experts - HOT
    hot_cap = 2 * tok_rows * top_count // experts
    cold_cap = (tok_rows * top_count - HOT * hot_cap + cold_count - 1) // cold_count
    capacity = max(hot_cap, cold_cap)
    local_rows = experts * capacity
    gate_matrix, up_matrix, down_matrix = w_gate[0], w_up[0], w_down[0]
    width = gate_matrix.shape[1]
    grid = (features // COLUMNS,)
    pick_scratch = [pltpu.VMEM((tok_rows, local_rows), BF16)]

    position, send_rows = call(
        functools.partial(dispatch_kernel, experts=experts, capacity=capacity),
        [fixed(routing), across(tokens)],
        [(routing.shape, jnp.int32, pl.BlockSpec(routing.shape, lambda i: (0, 0))), by_column(local_rows, features, BF16)],
        24,
        grid=grid,
        scratch=pick_scratch,
    )
    rows_own = exchange(send_rows, experts)
    targets = jnp.arange(local_rows, dtype=jnp.int32)
    selected = position[None, :, :] == targets[:, None, None]
    picker = jnp.any(selected, axis=2).astype(BF16)
    slot_weight = jnp.sum(jnp.where(selected, combine_weights[None, :, :], 0.0), axis=(1, 2))
    send_grads = (slot_weight[:, None] * dot(picker, cotangent, ((1,), (0,)))).astype(BF16)
    rows_own, send_grads = lax.optimization_barrier((rows_own, send_grads))
    grads_own = exchange(send_grads, experts)

    weights = [whole(matrix) for matrix in (gate_matrix, up_matrix, down_matrix)]
    kept = [out_whole((local_rows, width), kind) for kind in (BF16, F32, F32)]
    pair = [out_whole((local_rows, width), BF16)] * 2
    parts = [out_whole((local_rows // PARTS, features), BF16)] * PARTS
    send = [out_whole((local_rows, features), BF16)]

    rows_peer = swap(rows_own)
    hidden_own, act_own, slope_own = call(hidden_kernel, [whole(rows_own)] + weights[:2], kept, 32)
    hidden_peer, act_peer, slope_peer, *outs = call(forward_kernel, [whole(rows_peer)] + weights, kept + parts, 40)
    outs = [swap(out) for out in outs]
    (out_send,) = call(out_kernel, [whole(hidden_own)] + weights[2:] + [whole(out) for out in outs], send, 32)
    grads_own, out_send = lax.optimization_barrier((grads_own, out_send))
    out_back = exchange(out_send, experts)

    grads_peer = swap(grads_own)
    gate_own, up_own = call(
        grad_kernel, [whole(value) for value in (grads_own, act_own, slope_own)] + weights[2:], pair, 32
    )
    gate_peer, up_peer, *ins = call(
        backward_kernel, [whole(value) for value in (grads_peer, act_peer, slope_peer)] + weights, pair + parts, 40
    )
    ins = [swap(value) for value in ins]
    (input_send,) = call(
        input_kernel, [whole(gate_own), whole(up_own)] + weights[:2] + [whole(value) for value in ins], send, 32
    )
    out_back, input_send = lax.optimization_barrier((out_back, input_send))
    input_back = exchange(input_send, experts)

    wgrads = weight_grads(
        [rows_own, rows_peer, grads_own, grads_peer],
        [hidden_own, hidden_peer, gate_own, gate_peer, up_own, up_peer],
    )
    (combined,) = call(
        combine_kernel,
        [fixed(position), fixed(combine_weights), across(out_back)],
        [by_column(tok_rows, features, BF16)],
        24,
        grid=grid,
    )
    *wgrads, combined, input_back = lax.optimization_barrier((*wgrads, combined, input_back))
    (token_grad,) = call(
        token_grad_kernel,
        [fixed(position), across(input_back)],
        [by_column(tok_rows, features, BF16)],
        24,
        grid=grid,
        scratch=pick_scratch,
    )
    return combined, token_grad, wgrads[0][None], wgrads[1][None], wgrads[2][None]


def solution(mesh):
    in_specs = (
        P(("dp", "expert"), None),
        P(("dp", "expert"), None),
        P(("dp", "expert"), None),
        P(("dp", "expert"), None),
        P("expert", None, "dp"),
        P("expert", None, "dp"),
        P("expert", "dp", None),
    )
    out_specs = (
        P(("dp", "expert"), None),
        P(("dp", "expert"), None),
        P("expert", None, "dp"),
        P("expert", None, "dp"),
        P("expert", "dp", None),
    )
    return jax.shard_map(local, mesh=mesh, in_specs=in_specs, out_specs=out_specs, check_vma=False)
```

```python
import functools

import jax
import jax.numpy as jnp
from jax import lax
from jax.experimental import pallas as pl
from jax.experimental.pallas import tpu as pltpu
from jax.sharding import PartitionSpec as P

HOT = 4
COLUMNS = 512
BROAD = 1024
PARTS = 2
BF16 = jnp.bfloat16
F32 = jnp.float32
MIB = 1024 * 1024


def dot(left, right, dims):
    return lax.dot_general(left, right, (dims, ((), ())), preferred_element_type=F32)


def swap(value):
    return lax.ppermute(value, "dp", [(0, 1), (1, 0)])


def exchange(value, experts):
    rows, features = value.shape
    parts = value.reshape(experts, rows // experts, features)
    moved = lax.all_to_all(parts, "expert", split_axis=0, concat_axis=0, tiled=True)
    return moved.reshape(rows, features)


def call(kernel, args, outs, limit, grid=(), scratch=(), pinned=False):
    in_specs = [spec for _, spec in args]
    return pl.pallas_call(
        kernel,
        grid=grid,
        in_specs=in_specs,
        out_specs=[spec for _, _, spec in outs],
        out_shape=[(pltpu.HBM if pinned else jax.ShapeDtypeStruct)(shape, kind) for shape, kind, _ in outs],
        scratch_shapes=scratch,
        compiler_params=pltpu.CompilerParams(vmem_limit_bytes=limit * MIB),
        cost_estimate=pl.CostEstimate(flops=1000, bytes_accessed=1000, transcendentals=0),
    )(*[arg for arg, _ in args])


def whole(arg):
    return arg, pl.BlockSpec(memory_space=pltpu.VMEM)


def fixed(arg):
    return arg, pl.BlockSpec(arg.shape, lambda i: (0, 0))


def across(arg, columns):
    return arg, pl.BlockSpec((arg.shape[0], columns), lambda i: (0, i))


def out_whole(shape, kind):
    return shape, kind, pl.BlockSpec(memory_space=pltpu.VMEM)


def by_column(rows, columns, kind, wide):
    return (rows, columns), kind, pl.BlockSpec((rows, wide), lambda i: (0, i))


def joined(refs):
    return jnp.concatenate([ref[...] for ref in refs], axis=0)


def hidden_parts(rows, gate_matrix, up_matrix):
    gate_pre = dot(rows, gate_matrix, ((1,), (0,)))
    up_pre = dot(rows, up_matrix, ((1,), (0,)))
    sig_gate = jax.nn.sigmoid(gate_pre)
    activated = gate_pre * sig_gate
    hidden = (activated * up_pre).astype(BF16)
    gate_slope = up_pre * sig_gate * (1.0 + gate_pre * (1.0 - sig_gate))
    return hidden, activated, gate_slope


def grad_parts(grads, act, slope, down_matrix):
    hidden_grad = dot(grads, down_matrix, ((1,), (1,)))
    return (hidden_grad * slope).astype(BF16), (hidden_grad * act).astype(BF16)


def input_parts(gate_grad, up_grad, gate_matrix, up_matrix):
    return dot(gate_grad, gate_matrix, ((1,), (1,))) + dot(up_grad, up_matrix, ((1,), (1,)))


def places(routing_ref, position_ref, experts, capacity):
    top_count, tok_rows = routing_ref.shape
    expert_ids = lax.broadcasted_iota(jnp.int32, (experts, tok_rows), 0)
    named = [routing_ref[column : column + 1] == expert_ids for column in range(top_count)]
    counts = sum(hit.astype(F32) for hit in named)
    earlier = lax.broadcasted_iota(jnp.int32, (tok_rows, tok_rows), 0) < lax.broadcasted_iota(
        jnp.int32, (tok_rows, tok_rows), 1
    )
    before = dot(counts.astype(BF16), earlier.astype(F32).astype(BF16), ((1,), (0,)))
    for column, hit in enumerate(named):
        slot = jnp.sum(jnp.where(hit, before, 0.0), axis=0, keepdims=True).astype(jnp.int32)
        position_ref[column : column + 1] = routing_ref[column : column + 1] * capacity + slot


def dispatch_kernel(routing_ref, tokens_ref, position_ref, out_ref, pick_ref, *, experts, capacity):
    @pl.when(pl.program_id(0) == 0)
    def _():
        places(routing_ref, position_ref, experts, capacity)
        slots = lax.broadcasted_iota(jnp.int32, pick_ref.shape, 0)
        hits = [position_ref[column : column + 1] == slots for column in range(position_ref.shape[0])]
        pick_ref[...] = sum(hit.astype(F32) for hit in hits).astype(BF16)

    out_ref[...] = dot(pick_ref[...], tokens_ref[...], ((1,), (0,))).astype(BF16)


def pick_matrix(position_ref, local_rows):
    tok_rows, top_count = position_ref.shape
    slots = lax.broadcasted_iota(jnp.int32, (tok_rows, local_rows), 1)
    return sum((position_ref[:, column : column + 1] == slots).astype(F32) for column in range(top_count)).astype(BF16)


def token_grad_kernel(position_ref, rows_ref, out_ref, pick_ref):
    @pl.when(pl.program_id(0) == 0)
    def _():
        pick_ref[...] = pick_matrix(position_ref, pick_ref.shape[1])

    out_ref[...] = dot(pick_ref[...], rows_ref[...], ((1,), (0,))).astype(BF16)


def combine_kernel(position_ref, weight_ref, rows_ref, out_ref):
    rows = rows_ref[...]
    tok_rows, top_count = position_ref.shape
    slots = lax.broadcasted_iota(jnp.int32, (tok_rows, rows.shape[0]), 1)
    total = jnp.zeros(out_ref.shape, F32)
    for column in range(top_count):
        pick = (position_ref[:, column : column + 1] == slots).astype(F32).astype(BF16)
        total += weight_ref[:, column : column + 1] * dot(pick, rows, ((1,), (0,)))
    out_ref[...] = total.astype(BF16)


def hidden_kernel(rows_ref, gate_ref, up_ref, hidden_ref, act_ref, slope_ref):
    hidden_ref[...], act_ref[...], slope_ref[...] = hidden_parts(rows_ref[...], gate_ref[...], up_ref[...])


def forward_kernel(rows_ref, gate_ref, up_ref, down_ref, hidden_ref, act_ref, slope_ref, *out_refs):
    hidden, act_ref[...], slope_ref[...] = hidden_parts(rows_ref[...], gate_ref[...], up_ref[...])
    hidden_ref[...] = hidden
    size = hidden.shape[0] // len(out_refs)
    for i, out_ref in enumerate(out_refs):
        out_ref[...] = dot(hidden[i * size : (i + 1) * size], down_ref[...], ((1,), (0,))).astype(BF16)


def out_kernel(hidden_ref, down_ref, *refs):
    peer_refs, out_ref = refs[:-1], refs[-1]
    size = hidden_ref.shape[0] // len(peer_refs)
    for i, peer_ref in enumerate(peer_refs):
        rows = slice(i * size, (i + 1) * size)
        total = dot(hidden_ref[rows], down_ref[...], ((1,), (0,))) + peer_ref[...].astype(F32)
        out_ref[rows] = total.astype(BF16)


def grad_kernel(grads_ref, act_ref, slope_ref, down_ref, gate_grad_ref, up_grad_ref):
    gate_grad_ref[...], up_grad_ref[...] = grad_parts(grads_ref[...], act_ref[...], slope_ref[...], down_ref[...])


def backward_kernel(grads_ref, act_ref, slope_ref, gate_ref, up_ref, down_ref, gate_grad_ref, up_grad_ref, *in_refs):
    gate_grad, up_grad = grad_parts(grads_ref[...], act_ref[...], slope_ref[...], down_ref[...])
    gate_grad_ref[...] = gate_grad
    up_grad_ref[...] = up_grad
    size = gate_grad.shape[0] // len(in_refs)
    for i, in_ref in enumerate(in_refs):
        rows = slice(i * size, (i + 1) * size)
        in_ref[...] = input_parts(gate_grad[rows], up_grad[rows], gate_ref[...], up_ref[...]).astype(BF16)


def input_kernel(gate_grad_ref, up_grad_ref, gate_ref, up_ref, *refs):
    peer_refs, out_ref = refs[:-1], refs[-1]
    size = gate_grad_ref.shape[0] // len(peer_refs)
    for i, peer_ref in enumerate(peer_refs):
        rows = slice(i * size, (i + 1) * size)
        total = input_parts(gate_grad_ref[rows], up_grad_ref[rows], gate_ref[...], up_ref[...])
        out_ref[rows] = (total + peer_ref[...].astype(F32)).astype(BF16)


def weight_kernel(*refs):
    rows, grads, hidden, gate_grad, up_grad = (refs[2 * i : 2 * i + 2] for i in range(5))
    gate_out, up_out, down_out = refs[10:]
    both = jnp.concatenate([joined(gate_grad), joined(up_grad)], axis=1)
    total = dot(joined(rows), both, ((0,), (0,)))
    width = gate_out.shape[1]
    gate_out[...] = total[:, :width].astype(BF16)
    up_out[...] = total[:, width:].astype(BF16)
    down_out[...] = dot(joined(hidden), joined(grads), ((0,), (0,))).astype(BF16)


def weight_grads(wide, kept):
    features = wide[0].shape[1]
    width = kept[0].shape[1]
    args = [(value, pl.BlockSpec((value.shape[0], COLUMNS), lambda i: (0, i))) for value in wide]
    args += [fixed(value) for value in kept]
    tall = ((features, width), BF16, pl.BlockSpec((COLUMNS, width), lambda i: (i, 0)))
    return call(weight_kernel, args, [tall, tall, by_column(width, features, BF16, COLUMNS)], 48, grid=(features // COLUMNS,))


def local(tokens, cotangent, routing, combine_weights, w_gate, w_up, w_down):
    tok_rows, features = tokens.shape
    top_count = routing.shape[1]
    experts = lax.axis_size("expert")
    cold_count = experts - HOT
    hot_cap = 2 * tok_rows * top_count // experts
    cold_cap = (tok_rows * top_count - HOT * hot_cap + cold_count - 1) // cold_count
    capacity = max(hot_cap, cold_cap)
    local_rows = experts * capacity
    gate_matrix, up_matrix, down_matrix = w_gate[0], w_up[0], w_down[0]
    width = gate_matrix.shape[1]
    broad_grid = (features // BROAD,)
    pick_scratch = [pltpu.VMEM((tok_rows, local_rows), BF16)]

    place_shape = (top_count, tok_rows)
    position, send_rows = call(
        functools.partial(dispatch_kernel, experts=experts, capacity=capacity),
        [fixed(routing.T), across(tokens, BROAD)],
        [(place_shape, jnp.int32, pl.BlockSpec(place_shape, lambda i: (0, 0))), by_column(local_rows, features, BF16, BROAD)],
        24,
        grid=broad_grid,
        scratch=[pltpu.VMEM((local_rows, tok_rows), BF16)],
        pinned=True,
    )
    position = position.T
    rows_own = exchange(send_rows, experts)
    targets = jnp.arange(local_rows, dtype=jnp.int32)
    selected = position[None, :, :] == targets[:, None, None]
    picker = jnp.any(selected, axis=2).astype(BF16)
    slot_weight = jnp.sum(jnp.where(selected, combine_weights[None, :, :], 0.0), axis=(1, 2))
    send_grads = (slot_weight[:, None] * dot(picker, cotangent, ((1,), (0,)))).astype(BF16)
    rows_own, send_grads = lax.optimization_barrier((rows_own, send_grads))
    grads_own = exchange(send_grads, experts)

    weights = [whole(matrix) for matrix in (gate_matrix, up_matrix, down_matrix)]
    kept = [out_whole((local_rows, width), kind) for kind in (BF16, F32, F32)]
    pair = [out_whole((local_rows, width), BF16)] * 2
    parts = [out_whole((local_rows // PARTS, features), BF16)] * PARTS
    send = [out_whole((local_rows, features), BF16)]

    rows_peer = swap(rows_own)
    hidden_own, act_own, slope_own = call(hidden_kernel, [whole(rows_own)] + weights[:2], kept, 32)
    hidden_peer, act_peer, slope_peer, *outs = call(forward_kernel, [whole(rows_peer)] + weights, kept + parts, 40)
    outs = [swap(out) for out in outs]
    (out_send,) = call(out_kernel, [whole(hidden_own)] + weights[2:] + [whole(out) for out in outs], send, 32)
    grads_own, out_send = lax.optimization_barrier((grads_own, out_send))
    out_back = exchange(out_send, experts)

    grads_peer = swap(grads_own)
    gate_own, up_own = call(
        grad_kernel, [whole(value) for value in (grads_own, act_own, slope_own)] + weights[2:], pair, 32
    )
    gate_peer, up_peer, *ins = call(
        backward_kernel, [whole(value) for value in (grads_peer, act_peer, slope_peer)] + weights, pair + parts, 40
    )
    ins = [swap(value) for value in ins]
    (input_send,) = call(
        input_kernel, [whole(gate_own), whole(up_own)] + weights[:2] + [whole(value) for value in ins], send, 32
    )
    out_back, input_send = lax.optimization_barrier((out_back, input_send))
    input_back = exchange(input_send, experts)

    wgrads = weight_grads(
        [rows_own, rows_peer, grads_own, grads_peer],
        [hidden_own, hidden_peer, gate_own, gate_peer, up_own, up_peer],
    )
    (combined,) = call(
        combine_kernel,
        [fixed(position), fixed(combine_weights), across(out_back, BROAD)],
        [by_column(tok_rows, features, BF16, BROAD)],
        24,
        grid=broad_grid,
    )
    *wgrads, combined, input_back = lax.optimization_barrier((*wgrads, combined, input_back))
    (token_grad,) = call(
        token_grad_kernel,
        [fixed(position), across(input_back, BROAD)],
        [by_column(tok_rows, features, BF16, BROAD)],
        24,
        grid=broad_grid,
        scratch=pick_scratch,
    )
    return combined, token_grad, wgrads[0][None], wgrads[1][None], wgrads[2][None]


def solution(mesh):
    in_specs = (
        P(("dp", "expert"), None),
        P(("dp", "expert"), None),
        P(("dp", "expert"), None),
        P(("dp", "expert"), None),
        P("expert", None, "dp"),
        P("expert", None, "dp"),
        P("expert", "dp", None),
    )
    out_specs = (
        P(("dp", "expert"), None),
        P(("dp", "expert"), None),
        P("expert", None, "dp"),
        P("expert", None, "dp"),
        P("expert", "dp", None),
    )
    return jax.shard_map(local, mesh=mesh, in_specs=in_specs, out_specs=out_specs, check_vma=False)
```

```python
import functools

import jax
import jax.numpy as jnp
from jax import lax
from jax.experimental import pallas as pl
from jax.experimental.pallas import tpu as pltpu
from jax.sharding import PartitionSpec as P

HOT = 4
SIDE = 4
COLUMNS = 512
BROAD = 1024
PARTS = 2
BF16 = jnp.bfloat16
F32 = jnp.float32
MIB = 1024 * 1024


def dot(left, right, dims):
    return lax.dot_general(left, right, (dims, ((), ())), preferred_element_type=F32)


def swap(value):
    return lax.ppermute(value, "dp", [(0, 1), (1, 0)])


def shift(value, axis, steps):
    pairs = []
    for chip in range(SIDE**3):
        place = [chip // SIDE**2, chip // SIDE % SIDE, chip % SIDE]
        place[axis] = (place[axis] + steps) % SIDE
        pairs.append((chip, (place[0] * SIDE + place[1]) * SIDE + place[2]))
    return lax.ppermute(value, "expert", pairs)


def pack(value, experts):
    rows, features = value.shape
    return value.reshape(experts, rows // experts * 4, features // 4)


def exchange(parts):
    return lax.all_to_all(parts, "expert", split_axis=0, concat_axis=0, tiled=True)


def unpack(parts):
    experts, rows, features = parts.shape
    return parts.reshape(experts * rows // 4, features * 4)


def after(value, other):
    return lax.optimization_barrier((value, other))[0]


def call(kernel, args, outs, limit, grid=(), scratch=(), pinned=False):
    in_specs = [spec for _, spec in args]
    return pl.pallas_call(
        kernel,
        grid=grid,
        in_specs=in_specs,
        out_specs=[spec for _, _, spec in outs],
        out_shape=[(pltpu.HBM if pinned else jax.ShapeDtypeStruct)(shape, kind) for shape, kind, _ in outs],
        scratch_shapes=scratch,
        compiler_params=pltpu.CompilerParams(vmem_limit_bytes=limit * MIB),
        cost_estimate=pl.CostEstimate(flops=1000, bytes_accessed=1000, transcendentals=0),
    )(*[arg for arg, _ in args])


def whole(arg):
    return arg, pl.BlockSpec(memory_space=pltpu.VMEM)


def fixed(arg):
    return arg, pl.BlockSpec(arg.shape, lambda i: (0, 0))


def across(arg, columns):
    return arg, pl.BlockSpec((arg.shape[0], columns), lambda i: (0, i))


def out_whole(shape, kind):
    return shape, kind, pl.BlockSpec(memory_space=pltpu.VMEM)


def by_column(rows, columns, kind, wide):
    return (rows, columns), kind, pl.BlockSpec((rows, wide), lambda i: (0, i))


def joined(refs, part=None):
    if part is None:
        return jnp.concatenate([ref[...] for ref in refs], axis=0)
    half = refs[0].shape[0] // 2
    return jnp.concatenate([ref[part * half : (part + 1) * half] for ref in refs], axis=0)


def hidden_parts(rows, gate_matrix, up_matrix):
    gate_pre = dot(rows, gate_matrix, ((1,), (0,)))
    up_pre = dot(rows, up_matrix, ((1,), (0,)))
    sig_gate = jax.nn.sigmoid(gate_pre)
    activated = gate_pre * sig_gate
    hidden = (activated * up_pre).astype(BF16)
    gate_slope = up_pre * sig_gate * (1.0 + gate_pre * (1.0 - sig_gate))
    return hidden, activated, gate_slope


def grad_parts(grads, act, slope, down_matrix):
    hidden_grad = dot(grads, down_matrix, ((1,), (1,)))
    return (hidden_grad * slope).astype(BF16), (hidden_grad * act).astype(BF16)


def input_parts(gate_grad, up_grad, gate_matrix, up_matrix):
    return dot(gate_grad, gate_matrix, ((1,), (1,))) + dot(up_grad, up_matrix, ((1,), (1,)))


def places(routing_ref, position_ref, experts, capacity, spare):
    top_count, tok_rows = routing_ref.shape
    expert_ids = lax.broadcasted_iota(jnp.int32, (experts, tok_rows), 0)
    named = [routing_ref[column : column + 1] == expert_ids for column in range(top_count)]
    counts = sum(hit.astype(F32) for hit in named)
    earlier = lax.broadcasted_iota(jnp.int32, (tok_rows, tok_rows), 0) < lax.broadcasted_iota(
        jnp.int32, (tok_rows, tok_rows), 1
    )
    before = dot(counts.astype(BF16), earlier.astype(F32).astype(BF16), ((1,), (0,)))
    is_hot = jnp.sum(counts, axis=1, keepdims=True) > capacity
    is_hot = jnp.broadcast_to(is_hot.astype(F32), counts.shape).astype(BF16)
    lower = lax.broadcasted_iota(jnp.int32, (experts, experts), 1) < lax.broadcasted_iota(
        jnp.int32, (experts, experts), 0
    )
    rank = dot(lower.astype(F32).astype(BF16), is_hot, ((1,), (0,)))
    for column, hit in enumerate(named):
        slot = jnp.sum(jnp.where(hit, before, 0.0), axis=0, keepdims=True).astype(jnp.int32)
        hot_rank = jnp.sum(jnp.where(hit, rank, 0.0), axis=0, keepdims=True).astype(jnp.int32)
        main = routing_ref[column : column + 1] * capacity + slot
        extra = experts * capacity + hot_rank * spare + slot - capacity
        position_ref[column : column + 1] = jnp.where(slot < capacity, main, extra)


def dispatch_kernel(
    routing_ref, weight_ref, tokens_ref, cotangent_ref, position_ref, out_ref, extra_ref, pick_ref, scale_ref, *, experts, capacity, spare
):
    main_count = experts * capacity
    extra_count = extra_ref.shape[0] // 2

    @pl.when(pl.program_id(0) == 0)
    def _():
        places(routing_ref, position_ref, experts, capacity, spare)
        slots = lax.broadcasted_iota(jnp.int32, pick_ref.shape, 0)
        extra_slots = lax.broadcasted_iota(jnp.int32, (extra_count, pick_ref.shape[1]), 0) + main_count
        pick = jnp.zeros(pick_ref.shape, F32)
        scale = jnp.zeros(extra_slots.shape, F32)
        for column in range(position_ref.shape[0]):
            position = position_ref[column : column + 1]
            pick += (position == slots).astype(F32)
            scale += jnp.where(position == extra_slots, weight_ref[column : column + 1], 0.0)
        pick_ref[...] = pick.astype(BF16)
        scale_ref[...] = jnp.broadcast_to(jnp.sum(scale, axis=1, keepdims=True), scale_ref.shape)

    pick = pick_ref[...]
    chosen = dot(pick, tokens_ref[...], ((1,), (0,)))
    out_ref[...] = chosen[:main_count].astype(BF16)
    grads = dot(pick[main_count:], cotangent_ref[...], ((1,), (0,)))[:extra_count] * scale_ref[:, :1]
    extra_ref[...] = jnp.concatenate([chosen[main_count : main_count + extra_count], grads], axis=0).astype(BF16)


def choose_kernel(select_ref, *refs):
    pieces, outs = refs[:SIDE], refs[SIDE:]
    chosen = dot(select_ref[...], joined(pieces), ((1,), (0,))).astype(BF16)
    rows = outs[0].shape[0]
    for i, out in enumerate(outs):
        out[...] = chosen[i * rows : (i + 1) * rows]


def choose(select, pieces, out_rows):
    features = pieces[0].shape[1]
    args = [fixed(select)] + [across(piece, BROAD) for piece in pieces]
    outs = [by_column(out_rows, features, BF16, BROAD)] * SIDE
    return call(choose_kernel, args, outs, 32, grid=(features // BROAD,), pinned=True)


def combine_kernel(position_ref, weight_ref, main_ref, *refs, part):
    extras, out_ref = refs[:SIDE], refs[SIDE]
    main = main_ref[...]
    extra = sum(ref[...].astype(F32) for ref in extras).astype(BF16)
    tok_rows, top_count = position_ref.shape
    main_ids = lax.broadcasted_iota(jnp.int32, (tok_rows, main.shape[0]), 1)
    half = extra.shape[0] // 2
    extra_ids = lax.broadcasted_iota(jnp.int32, (tok_rows, extra.shape[0]), 1) - part * half
    extra_ids = jnp.where((extra_ids >= 0) & (extra_ids < half), extra_ids + main.shape[0], -1)
    picks = []
    for column in range(top_count):
        position = position_ref[:, column : column + 1]
        picks.append([(position == ids).astype(F32) for ids in (main_ids, extra_ids)])
    if part == 1:
        picks = [[sum(pick) for pick in zip(*picks)]]
    total = jnp.zeros(out_ref.shape, F32)
    for column, pick in enumerate(picks):
        found = dot(pick[0].astype(BF16), main, ((1,), (0,))) + dot(pick[1].astype(BF16), extra, ((1,), (0,)))
        total += found if part == 1 else weight_ref[:, column : column + 1] * found
    out_ref[...] = total.astype(BF16)


def combine(position, weights, main, extras, part):
    tok_rows, features = position.shape[0], main.shape[1]
    args = [fixed(position), fixed(weights), across(main, BROAD)] + [across(extra, BROAD) for extra in extras]
    outs = [by_column(tok_rows, features, BF16, BROAD)]
    return call(functools.partial(combine_kernel, part=part), args, outs, 24, grid=(features // BROAD,))[0]


def hidden_kernel(rows_ref, gate_ref, up_ref, hidden_ref, act_ref, slope_ref):
    hidden_ref[...], act_ref[...], slope_ref[...] = hidden_parts(rows_ref[...], gate_ref[...], up_ref[...])


def forward_kernel(rows_ref, gate_ref, up_ref, down_ref, hidden_ref, act_ref, slope_ref, *out_refs):
    hidden, act_ref[...], slope_ref[...] = hidden_parts(rows_ref[...], gate_ref[...], up_ref[...])
    hidden_ref[...] = hidden
    size = hidden.shape[0] // len(out_refs)
    for i, out_ref in enumerate(out_refs):
        out_ref[...] = dot(hidden[i * size : (i + 1) * size], down_ref[...], ((1,), (0,))).astype(BF16)


def out_kernel(hidden_ref, down_ref, *refs):
    peer_refs, out_ref = refs[:-1], refs[-1]
    size = hidden_ref.shape[0] // len(peer_refs)
    for i, peer_ref in enumerate(peer_refs):
        rows = slice(i * size, (i + 1) * size)
        total = dot(hidden_ref[rows], down_ref[...], ((1,), (0,))) + peer_ref[...].astype(F32)
        out_ref[rows] = total.astype(BF16)


def grad_kernel(grads_ref, act_ref, slope_ref, down_ref, gate_grad_ref, up_grad_ref):
    gate_grad_ref[...], up_grad_ref[...] = grad_parts(grads_ref[...], act_ref[...], slope_ref[...], down_ref[...])


def backward_kernel(grads_ref, act_ref, slope_ref, gate_ref, up_ref, down_ref, gate_grad_ref, up_grad_ref, *in_refs):
    gate_grad, up_grad = grad_parts(grads_ref[...], act_ref[...], slope_ref[...], down_ref[...])
    gate_grad_ref[...] = gate_grad
    up_grad_ref[...] = up_grad
    size = gate_grad.shape[0] // len(in_refs)
    for i, in_ref in enumerate(in_refs):
        rows = slice(i * size, (i + 1) * size)
        in_ref[...] = input_parts(gate_grad[rows], up_grad[rows], gate_ref[...], up_ref[...]).astype(BF16)


def input_kernel(gate_grad_ref, up_grad_ref, gate_ref, up_ref, *refs):
    peer_refs, out_ref = refs[:-1], refs[-1]
    size = gate_grad_ref.shape[0] // len(peer_refs)
    for i, peer_ref in enumerate(peer_refs):
        rows = slice(i * size, (i + 1) * size)
        total = input_parts(gate_grad_ref[rows], up_grad_ref[rows], gate_ref[...], up_ref[...])
        out_ref[rows] = (total + peer_ref[...].astype(F32)).astype(BF16)


def extra_kernel(*refs):
    blocks, (gate_ref, up_ref, down_ref, hidden_ref, gate_grad_ref, up_grad_ref) = refs[:8], refs[8:14]
    sends = refs[14:]
    hidden, act, slope = hidden_parts(joined(blocks, 0), gate_ref[...], up_ref[...])
    gate_grad, up_grad = grad_parts(joined(blocks, 1), act, slope, down_ref[...])
    hidden_ref[...], gate_grad_ref[...], up_grad_ref[...] = hidden, gate_grad, up_grad
    own = hidden.shape[0] // 2
    out = dot(hidden[own:], down_ref[...], ((1,), (0,))).astype(BF16)
    back = input_parts(gate_grad[own:], up_grad[own:], gate_ref[...], up_ref[...]).astype(BF16)
    half = sends[0].shape[0] // 2
    for i, send in enumerate(sends):
        send[:half] = out[i * half : (i + 1) * half]
        send[half:] = back[i * half : (i + 1) * half]


def extra_out_kernel(*refs):
    hidden_ref, gate_grad_ref, up_grad_ref, gate_ref, up_ref, down_ref = refs[:6]
    peers, sends = refs[6:10], refs[10:]
    own = hidden_ref.shape[0] // 2
    out = dot(hidden_ref[:own], down_ref[...], ((1,), (0,)))
    back = input_parts(gate_grad_ref[:own], up_grad_ref[:own], gate_ref[...], up_ref[...])
    half = sends[0].shape[0] // 2
    for i, (peer, send) in enumerate(zip(peers, sends)):
        send[:half] = (out[i * half : (i + 1) * half] + peer[:half].astype(F32)).astype(BF16)
        send[half:] = (back[i * half : (i + 1) * half] + peer[half:].astype(F32)).astype(BF16)


def weight_kernel(*refs, wide):
    rows, grads = refs[:wide], refs[wide : 2 * wide]
    hidden, gate_grad, up_grad = (refs[2 * wide + 3 * i : 2 * wide + 3 * i + 3] for i in range(3))
    gate_out, up_out, down_out = refs[2 * wide + 9 :]
    both = jnp.concatenate([joined(gate_grad), joined(up_grad)], axis=1)
    total = dot(joined(rows), both, ((0,), (0,)))
    width = gate_out.shape[1]
    gate_out[...] = total[:, :width].astype(BF16)
    up_out[...] = total[:, width:].astype(BF16)
    down_out[...] = dot(joined(hidden), joined(grads), ((0,), (0,))).astype(BF16)


def weight_grads(main_rows, main_grads, blocks, kept):
    features = main_rows[0].shape[1]
    width = kept[0].shape[1]
    half = blocks[0].shape[0] // 2
    args = []
    for part, mains in enumerate((main_rows, main_grads)):
        args += [across(main, COLUMNS) for main in mains]
        args += [(block, pl.BlockSpec((half, COLUMNS), lambda i, part=part: (part, i))) for block in blocks]
    args += [fixed(value) for value in kept]
    tall = ((features, width), BF16, pl.BlockSpec((COLUMNS, width), lambda i: (i, 0)))
    outs = [tall, tall, by_column(width, features, BF16, COLUMNS)]
    kernel = functools.partial(weight_kernel, wide=len(main_rows) + len(blocks))
    return call(kernel, args, outs, 48, grid=(features // COLUMNS,))


def digits(count, sizes):
    ids = jnp.arange(count, dtype=jnp.int32)
    found = []
    for size in reversed(sizes):
        found.append(ids % size)
        ids = ids // size
    return found[::-1]


def local(tokens, cotangent, routing, combine_weights, w_gate, w_up, w_down):
    tok_rows, features = tokens.shape
    top_count = routing.shape[1]
    experts = lax.axis_size("expert")
    cold_count = experts - HOT
    hot_cap = 2 * tok_rows * top_count // experts
    cold_cap = (tok_rows * top_count - HOT * hot_cap + cold_count - 1) // cold_count
    capacity = (hot_cap + cold_cap) // 2
    spare = hot_cap - capacity
    main_count = experts * capacity
    extra_count = HOT * spare
    gate_matrix, up_matrix, down_matrix = w_gate[0], w_up[0], w_down[0]
    width = gate_matrix.shape[1]

    place_shape = (top_count, tok_rows)
    padded = main_count + 2 * extra_count
    position, send_rows, along_x = call(
        functools.partial(dispatch_kernel, experts=experts, capacity=capacity, spare=spare),
        [fixed(routing.T), fixed(combine_weights.T), across(tokens, BROAD), across(cotangent, BROAD)],
        [
            (place_shape, jnp.int32, pl.BlockSpec(place_shape, lambda i: (0, 0))),
            by_column(main_count, features, BF16, BROAD),
            by_column(2 * extra_count, features, BF16, BROAD),
        ],
        24,
        grid=(features // BROAD,),
        scratch=[pltpu.VMEM((padded, tok_rows), BF16), pltpu.VMEM((extra_count, 128), F32)],
        pinned=True,
    )
    position = position.T
    rows_own = exchange(pack(send_rows, experts))

    expert_ids = jnp.arange(experts, dtype=jnp.int32)
    matches = (routing.reshape(-1)[:, None] == expert_ids[None, :]).astype(jnp.int32)
    is_hot = (jnp.sum(matches, axis=0) > capacity).astype(jnp.int32)
    hot_rank = jnp.sum(jnp.where(expert_ids[None, :] < expert_ids[:, None], is_hot[None, :], 0), axis=1)
    rank_ids = jnp.where(is_hot > 0, hot_rank, -1)
    targets = jnp.arange(main_count, dtype=jnp.int32)
    selected = position[None, :, :] == targets[:, None, None]
    picker = jnp.any(selected, axis=2).astype(BF16)
    slot_weight = jnp.sum(jnp.where(selected, combine_weights[None, :, :], 0.0), axis=(1, 2))
    send_grads = (slot_weight[:, None] * dot(picker, cotangent, ((1,), (0,)))).astype(BF16)

    me = lax.axis_index("expert")
    here = [me // SIDE**2, me // SIDE % SIDE, me % SIDE]
    along_y = jnp.concatenate([along_x] + [shift(along_x, 2, step) for step in range(1, SIDE)])
    pieces = [along_y] + [shift(along_y, 1, step) for step in range(1, SIDE)]
    gathered = SIDE * SIDE * 2 * extra_count
    out_z, out_t, out_y, out_x, out_r = digits(gathered, (SIDE, 2, SIDE, SIDE, spare))
    in_y, in_x, in_t, in_h, in_r = digits(gathered, (SIDE, SIDE, 2, HOT, spare))
    steps = jnp.arange(SIDE, dtype=jnp.int32)
    line = ((here[0] + steps) % SIDE) * SIDE**2 + here[1] * SIDE + here[2]
    line_rank = jnp.sum(jnp.where(expert_ids[None, :] == line[:, None], rank_ids[None, :], 0), axis=1)
    out_rank = jnp.sum(jnp.where(out_z[:, None] == steps[None, :], line_rank[None, :], 0), axis=1)
    source = (out_y * SIDE + out_x) * 2 + out_t
    origin = (in_y * SIDE + in_x) * 2 + in_t
    to_line = (
        ((source * spare + out_r)[:, None] == (origin * spare + in_r)[None, :]) & (out_rank[:, None] == in_h[None, :])
    ).astype(BF16)
    send_grads = pack(send_grads, experts)
    rows_own, send_grads, *pieces = lax.optimization_barrier((rows_own, send_grads, *pieces))
    rows_own = unpack(rows_own)
    grads_own = exchange(send_grads)
    blocks = choose(to_line, pieces, gathered // SIDE)
    blocks = [blocks[0]] + [shift(blocks[step], 0, step) for step in range(1, SIDE)]
    peer_blocks = [swap(block) for block in blocks]


    weights = [whole(matrix) for matrix in (gate_matrix, up_matrix, down_matrix)]
    kept = [out_whole((main_count, width), kind) for kind in (BF16, F32, F32)]
    pair = [out_whole((main_count, width), BF16)] * 2
    parts = [out_whole((main_count // PARTS, features), BF16)] * PARTS
    send = [out_whole((main_count, features), BF16)]
    rows_peer = swap(rows_own)
    hidden_own, act_own, slope_own = call(hidden_kernel, [whole(rows_own)] + weights[:2], kept, 32)
    hidden_peer, act_peer, slope_peer, *outs = call(forward_kernel, [whole(rows_peer)] + weights, kept + parts, 40)
    outs = [swap(out) for out in outs]
    (out_send,) = call(out_kernel, [whole(hidden_own)] + weights[2:] + [whole(out) for out in outs], send, 32)

    out_send = pack(out_send, experts)

    extra_both = 2 * SIDE**3 * spare
    block_shape = blocks[0].shape
    hidden_e, gate_e, up_e, *sends = call(
        extra_kernel,
        [whole(block) for block in [after(blocks[0], out_send)] + blocks[1:] + peer_blocks] + weights,
        [out_whole((extra_both, width), BF16)] * 3 + [out_whole(block_shape, BF16)] * SIDE,
        56,
    )
    grads_own, out_send, *sends = lax.optimization_barrier((grads_own, out_send, *sends))
    grads_own = unpack(grads_own)
    out_back = exchange(out_send)

    grads_peer = swap(grads_own)
    gate_own, up_own = call(
        grad_kernel, [whole(value) for value in (grads_own, act_own, slope_own)] + weights[2:], pair, 32
    )
    gate_peer, up_peer, *ins = call(
        backward_kernel, [whole(value) for value in (grads_peer, act_peer, slope_peer)] + weights, pair + parts, 40
    )
    ins = [swap(value) for value in ins]
    (input_send,) = call(
        input_kernel, [whole(gate_own), whole(up_own)] + weights[:2] + [whole(value) for value in ins], send, 32
    )

    input_send = pack(input_send, experts)

    peers = [swap(send) for send in sends]
    peers[0] = after(peers[0], gate_peer)
    backs = call(
        extra_out_kernel,
        [whole(value) for value in (hidden_e, gate_e, up_e)] + weights + [whole(peer) for peer in peers],
        [out_whole(block_shape, BF16)] * SIDE,
        48,
    )

    backs = [backs[0]] + [shift(backs[step], 0, -step) for step in range(1, SIDE)]
    out_back, input_send, *backs = lax.optimization_barrier((out_back, input_send, *backs))
    out_back = unpack(out_back)
    input_back = exchange(input_send)
    group = SIDE * spare
    back_half = block_shape[0] // 2
    planes = []
    for step in range(SIDE):
        rows = [
            back[part * back_half + step * group : part * back_half + (step + 1) * group]
            for back in backs
            for part in range(2)
        ]
        plane = jnp.concatenate(rows)
        planes.append(plane if step == 0 else shift(plane, 1, -step))
    home_x, home_t, home_h, home_r = digits(SIDE * 2 * extra_count, (SIDE, 2, HOT, spare))
    in_y, in_z, in_t, in_x, in_r = digits(gathered, (SIDE, SIDE, 2, SIDE, spare))
    ranks = jnp.arange(HOT, dtype=jnp.int32)
    hot_ids = jnp.sum(jnp.where(rank_ids[None, :] == ranks[:, None], expert_ids[None, :], 0), axis=1)
    hot_step_y = (hot_ids // SIDE % SIDE - here[1]) % SIDE
    hot_step_z = (hot_ids // SIDE**2 - here[0]) % SIDE
    hot_here = jnp.where(hot_ids % SIDE == here[2], hot_step_y * SIDE + hot_step_z, -1)
    home_from = jnp.sum(jnp.where(home_h[:, None] == ranks[None, :], hot_here[None, :], 0), axis=1)
    to_home = (
        (((home_t * SIDE + home_x) * spare + home_r)[:, None] == ((in_t * SIDE + in_x) * spare + in_r)[None, :])
        & (home_from[:, None] == (in_y * SIDE + in_z)[None, :])
    ).astype(BF16)
    wgrads = weight_grads(
        [rows_own, rows_peer],
        [grads_own, grads_peer],
        blocks + peer_blocks,
        [hidden_own, hidden_peer, hidden_e, gate_own, gate_peer, gate_e, up_own, up_peer, up_e],
    )
    planes[0] = after(planes[0], wgrads[2])
    lasts = choose(to_home, planes, 2 * extra_count)
    lasts = [lasts[0]] + [shift(lasts[step], 2, -step) for step in range(1, SIDE)]


    combined = combine(position, combine_weights, out_back, lasts, 0)
    *wgrads, combined, input_back = lax.optimization_barrier((*wgrads, combined, input_back))
    token_grad = combine(position, combine_weights, unpack(input_back), lasts, 1)
    return combined, token_grad, wgrads[0][None], wgrads[1][None], wgrads[2][None]


def solution(mesh):
    in_specs = (
        P(("dp", "expert"), None),
        P(("dp", "expert"), None),
        P(("dp", "expert"), None),
        P(("dp", "expert"), None),
        P("expert", None, "dp"),
        P("expert", None, "dp"),
        P("expert", "dp", None),
    )
    out_specs = (
        P(("dp", "expert"), None),
        P(("dp", "expert"), None),
        P("expert", None, "dp"),
        P("expert", None, "dp"),
        P("expert", "dp", None),
    )
    return jax.shard_map(local, mesh=mesh, in_specs=in_specs, out_specs=out_specs, check_vma=False)
```

```python
import functools

import jax
import jax.numpy as jnp
from jax import lax
from jax.experimental import pallas as pl
from jax.experimental.pallas import tpu as pltpu
from jax.sharding import PartitionSpec as P

HOT = 4
COLUMNS = 512
BROAD = 2048
PARTS = 2
BF16 = jnp.bfloat16
F32 = jnp.float32
MIB = 1024 * 1024


def dot(left, right, dims):
    return lax.dot_general(left, right, (dims, ((), ())), preferred_element_type=F32)


def swap(value):
    return lax.ppermute(value, "dp", [(0, 1), (1, 0)])


def exchange(value, experts):
    rows, features = value.shape
    parts = value.reshape(experts, rows // experts, features)
    moved = lax.all_to_all(parts, "expert", split_axis=0, concat_axis=0, tiled=True)
    return moved.reshape(rows, features)


def call(kernel, args, outs, limit, grid=(), scratch=(), pinned=False):
    in_specs = [spec for _, spec in args]
    return pl.pallas_call(
        kernel,
        grid=grid,
        in_specs=in_specs,
        out_specs=[spec for _, _, spec in outs],
        out_shape=[(pltpu.HBM if pinned else jax.ShapeDtypeStruct)(shape, kind) for shape, kind, _ in outs],
        scratch_shapes=scratch,
        compiler_params=pltpu.CompilerParams(vmem_limit_bytes=limit * MIB),
        cost_estimate=pl.CostEstimate(flops=1000, bytes_accessed=1000, transcendentals=0),
    )(*[arg for arg, _ in args])


def pin(arg):
    return pltpu.with_memory_space_constraint(arg, pltpu.HBM)


def whole(arg):
    return arg, pl.BlockSpec(memory_space=pltpu.VMEM)


def fixed(arg):
    return arg, pl.BlockSpec(arg.shape, lambda i: (0, 0))


def across(arg, columns):
    return arg, pl.BlockSpec((arg.shape[0], columns), lambda i: (0, i))


def out_whole(shape, kind):
    return shape, kind, pl.BlockSpec(memory_space=pltpu.VMEM)


def by_column(rows, columns, kind, wide):
    return (rows, columns), kind, pl.BlockSpec((rows, wide), lambda i: (0, i))


def joined(refs):
    return jnp.concatenate([ref[...] for ref in refs], axis=0)


def hidden_parts(rows, gate_matrix, up_matrix):
    gate_pre = dot(rows, gate_matrix, ((1,), (0,)))
    up_pre = dot(rows, up_matrix, ((1,), (0,)))
    sig_gate = jax.nn.sigmoid(gate_pre)
    activated = gate_pre * sig_gate
    hidden = (activated * up_pre).astype(BF16)
    gate_slope = up_pre * sig_gate * (1.0 + gate_pre * (1.0 - sig_gate))
    return hidden, activated, gate_slope


def grad_parts(grads, act, slope, down_matrix):
    hidden_grad = dot(grads, down_matrix, ((1,), (1,)))
    return (hidden_grad * slope).astype(BF16), (hidden_grad * act).astype(BF16)


def input_parts(gate_grad, up_grad, gate_matrix, up_matrix):
    return dot(gate_grad, gate_matrix, ((1,), (1,))) + dot(up_grad, up_matrix, ((1,), (1,)))


def places(routing_ref, position_ref, experts, capacity):
    top_count, tok_rows = routing_ref.shape
    expert_ids = lax.broadcasted_iota(jnp.int32, (experts, tok_rows), 0)
    named = [routing_ref[column : column + 1] == expert_ids for column in range(top_count)]
    counts = sum(hit.astype(F32) for hit in named)
    earlier = lax.broadcasted_iota(jnp.int32, (tok_rows, tok_rows), 0) < lax.broadcasted_iota(
        jnp.int32, (tok_rows, tok_rows), 1
    )
    before = dot(counts.astype(BF16), earlier.astype(F32).astype(BF16), ((1,), (0,)))
    for column, hit in enumerate(named):
        slot = jnp.sum(jnp.where(hit, before, 0.0), axis=0, keepdims=True).astype(jnp.int32)
        position_ref[column : column + 1] = routing_ref[column : column + 1] * capacity + slot


def dispatch_kernel(
    routing_ref, weight_ref, tokens_ref, cotangent_ref, position_ref, kept_ref, rows_ref, grads_ref, pick_ref, scale_ref, *, experts, capacity
):
    @pl.when(pl.program_id(0) == 0)
    def _():
        places(routing_ref, position_ref, experts, capacity)
        kept_ref[...] = weight_ref[...]
        slots = lax.broadcasted_iota(jnp.int32, pick_ref.shape, 0)
        columns = range(position_ref.shape[0])
        hits = [position_ref[column : column + 1] == slots for column in columns]
        pick_ref[...] = sum(hit.astype(F32) for hit in hits).astype(BF16)
        scale = sum(jnp.where(hits[column], weight_ref[column : column + 1], 0.0) for column in columns)
        scale_ref[...] = jnp.broadcast_to(jnp.sum(scale, axis=1, keepdims=True), scale_ref.shape)

    rows_ref[...] = dot(pick_ref[...], tokens_ref[...], ((1,), (0,))).astype(BF16)
    grads = dot(pick_ref[...], cotangent_ref[...], ((1,), (0,)))
    grads_ref[...] = (scale_ref[:, :1] * grads).astype(BF16)


def combine_kernel(position_ref, weight_ref, out_ref, input_ref, combined_ref, token_grad_ref, pick_ref):
    tok_rows, top_count = position_ref.shape

    @pl.when(pl.program_id(0) == 0)
    def _():
        slots = lax.broadcasted_iota(jnp.int32, (tok_rows, pick_ref.shape[1]), 1)
        picks = [(position_ref[:, column : column + 1] == slots).astype(F32) for column in range(top_count)]
        for column, pick in enumerate(picks + [sum(picks)]):
            pick_ref[column * tok_rows : (column + 1) * tok_rows] = pick.astype(BF16)

    found = dot(pick_ref[: top_count * tok_rows], out_ref[...], ((1,), (0,)))
    total = jnp.zeros(combined_ref.shape, F32)
    for column in range(top_count):
        total += weight_ref[:, column : column + 1] * found[column * tok_rows : (column + 1) * tok_rows]
    combined_ref[...] = total.astype(BF16)
    token_grad_ref[...] = dot(pick_ref[top_count * tok_rows :], input_ref[...], ((1,), (0,))).astype(BF16)


def hidden_kernel(rows_ref, gate_ref, up_ref, hidden_ref, act_ref, slope_ref):
    hidden_ref[...], act_ref[...], slope_ref[...] = hidden_parts(rows_ref[...], gate_ref[...], up_ref[...])


def forward_kernel(rows_ref, gate_ref, up_ref, down_ref, hidden_ref, act_ref, slope_ref, *out_refs):
    hidden, act_ref[...], slope_ref[...] = hidden_parts(rows_ref[...], gate_ref[...], up_ref[...])
    hidden_ref[...] = hidden
    size = hidden.shape[0] // len(out_refs)
    for i, out_ref in enumerate(out_refs):
        out_ref[...] = dot(hidden[i * size : (i + 1) * size], down_ref[...], ((1,), (0,))).astype(BF16)


def out_kernel(hidden_ref, down_ref, *refs):
    peer_refs, out_ref = refs[:-1], refs[-1]
    size = hidden_ref.shape[0] // len(peer_refs)
    for i, peer_ref in enumerate(peer_refs):
        rows = slice(i * size, (i + 1) * size)
        total = dot(hidden_ref[rows], down_ref[...], ((1,), (0,))) + peer_ref[...].astype(F32)
        out_ref[rows] = total.astype(BF16)


def grad_kernel(grads_ref, act_ref, slope_ref, down_ref, gate_grad_ref, up_grad_ref):
    gate_grad_ref[...], up_grad_ref[...] = grad_parts(grads_ref[...], act_ref[...], slope_ref[...], down_ref[...])


def backward_kernel(grads_ref, act_ref, slope_ref, gate_ref, up_ref, down_ref, gate_grad_ref, up_grad_ref, *in_refs):
    gate_grad, up_grad = grad_parts(grads_ref[...], act_ref[...], slope_ref[...], down_ref[...])
    gate_grad_ref[...] = gate_grad
    up_grad_ref[...] = up_grad
    size = gate_grad.shape[0] // len(in_refs)
    for i, in_ref in enumerate(in_refs):
        rows = slice(i * size, (i + 1) * size)
        in_ref[...] = input_parts(gate_grad[rows], up_grad[rows], gate_ref[...], up_ref[...]).astype(BF16)


def input_kernel(gate_grad_ref, up_grad_ref, gate_ref, up_ref, *refs):
    peer_refs, out_ref = refs[:-1], refs[-1]
    size = gate_grad_ref.shape[0] // len(peer_refs)
    for i, peer_ref in enumerate(peer_refs):
        rows = slice(i * size, (i + 1) * size)
        total = input_parts(gate_grad_ref[rows], up_grad_ref[rows], gate_ref[...], up_ref[...])
        out_ref[rows] = (total + peer_ref[...].astype(F32)).astype(BF16)


def weight_kernel(*refs):
    rows, grads, hidden, gate_grad, up_grad = (refs[2 * i : 2 * i + 2] for i in range(5))
    gate_out, up_out, down_out = refs[10:]
    both = jnp.concatenate([joined(gate_grad), joined(up_grad)], axis=1)
    total = dot(joined(rows), both, ((0,), (0,)))
    width = gate_out.shape[1]
    gate_out[...] = total[:, :width].astype(BF16)
    up_out[...] = total[:, width:].astype(BF16)
    down_out[...] = dot(joined(hidden), joined(grads), ((0,), (0,))).astype(BF16)


def weight_grads(wide, kept):
    features = wide[0].shape[1]
    width = kept[0].shape[1]
    args = [(value, pl.BlockSpec((value.shape[0], COLUMNS), lambda i: (0, i))) for value in wide]
    args += [fixed(value) for value in kept]
    tall = ((features, width), BF16, pl.BlockSpec((COLUMNS, width), lambda i: (i, 0)))
    return call(weight_kernel, args, [tall, tall, by_column(width, features, BF16, COLUMNS)], 48, grid=(features // COLUMNS,))


def local(tokens, cotangent, routing, combine_weights, w_gate, w_up, w_down):
    tok_rows, features = tokens.shape
    top_count = routing.shape[1]
    experts = lax.axis_size("expert")
    cold_count = experts - HOT
    hot_cap = 2 * tok_rows * top_count // experts
    cold_cap = (tok_rows * top_count - HOT * hot_cap + cold_count - 1) // cold_count
    capacity = max(hot_cap, cold_cap)
    local_rows = experts * capacity
    gate_matrix, up_matrix, down_matrix = w_gate[0], w_up[0], w_down[0]
    width = gate_matrix.shape[1]
    broad_grid = (features // BROAD,)
    place_shape = (top_count, tok_rows)
    sent = by_column(local_rows, features, BF16, BROAD)
    position, route_weights, send_rows, send_grads = call(
        functools.partial(dispatch_kernel, experts=experts, capacity=capacity),
        [fixed(routing.T), fixed(combine_weights.T), across(pin(tokens), BROAD), across(pin(cotangent), BROAD)],
        [(place_shape, kind, pl.BlockSpec(place_shape, lambda i: (0, 0))) for kind in (jnp.int32, F32)] + [sent, sent],
        40,
        grid=broad_grid,
        scratch=[pltpu.VMEM((local_rows, tok_rows), BF16), pltpu.VMEM((local_rows, 128), F32)],
        pinned=True,
    )
    rows_own = exchange(send_rows, experts)
    rows_own, send_grads, position, route_weights = lax.optimization_barrier(
        (rows_own, send_grads, position, route_weights)
    )
    position, route_weights = position.T, route_weights.T
    grads_own = exchange(send_grads, experts)

    weights = [whole(matrix) for matrix in (gate_matrix, up_matrix, down_matrix)]
    kept = [out_whole((local_rows, width), kind) for kind in (BF16, F32, F32)]
    pair = [out_whole((local_rows, width), BF16)] * 2
    parts = [out_whole((local_rows // PARTS, features), BF16)] * PARTS
    send = [out_whole((local_rows, features), BF16)]

    rows_peer = swap(rows_own)
    hidden_own, act_own, slope_own = call(hidden_kernel, [whole(rows_own)] + weights[:2], kept, 32)
    hidden_peer, act_peer, slope_peer, *outs = call(forward_kernel, [whole(rows_peer)] + weights, kept + parts, 40)
    outs = [swap(out) for out in outs]
    (out_send,) = call(out_kernel, [whole(hidden_own)] + weights[2:] + [whole(out) for out in outs], send, 32)
    grads_own, out_send = lax.optimization_barrier((grads_own, out_send))
    out_back = exchange(out_send, experts)

    grads_peer = swap(grads_own)
    gate_own, up_own = call(
        grad_kernel, [whole(value) for value in (grads_own, act_own, slope_own)] + weights[2:], pair, 32
    )
    gate_peer, up_peer, *ins = call(
        backward_kernel, [whole(value) for value in (grads_peer, act_peer, slope_peer)] + weights, pair + parts, 40
    )
    ins = [swap(value) for value in ins]
    (input_send,) = call(
        input_kernel, [whole(gate_own), whole(up_own)] + weights[:2] + [whole(value) for value in ins], send, 32
    )
    wgrads = weight_grads(
        [rows_own, rows_peer, grads_own, grads_peer],
        [hidden_own, hidden_peer, gate_own, gate_peer, up_own, up_peer],
    )
    out_back, input_send, position, route_weights, *wgrads = lax.optimization_barrier(
        (out_back, input_send, position, route_weights, *wgrads)
    )
    input_back = exchange(input_send, experts)
    combined, token_grad = call(
        combine_kernel,
        [fixed(position), fixed(route_weights), across(out_back, BROAD), across(input_back, BROAD)],
        [by_column(tok_rows, features, BF16, BROAD)] * 2,
        40,
        grid=broad_grid,
        scratch=[pltpu.VMEM(((top_count + 1) * tok_rows, local_rows), BF16)],
    )
    return combined, token_grad, wgrads[0][None], wgrads[1][None], wgrads[2][None]


def solution(mesh):
    in_specs = (
        P(("dp", "expert"), None),
        P(("dp", "expert"), None),
        P(("dp", "expert"), None),
        P(("dp", "expert"), None),
        P("expert", None, "dp"),
        P("expert", None, "dp"),
        P("expert", "dp", None),
    )
    out_specs = (
        P(("dp", "expert"), None),
        P(("dp", "expert"), None),
        P("expert", None, "dp"),
        P("expert", None, "dp"),
        P("expert", "dp", None),
    )
    return jax.shard_map(local, mesh=mesh, in_specs=in_specs, out_specs=out_specs, check_vma=False)
```

```python
import functools

import jax
import jax.numpy as jnp
from jax import lax
from jax.experimental import pallas as pl
from jax.experimental.pallas import tpu as pltpu
from jax.sharding import PartitionSpec as P

HOT = 4
COLUMNS = 512
BROAD = 2048
PARTS = 2
STEPS = 4
BF16 = jnp.bfloat16
F32 = jnp.float32
MIB = 1024 * 1024


def dot(left, right, dims):
    return lax.dot_general(left, right, (dims, ((), ())), preferred_element_type=F32)


def swap(value):
    return lax.ppermute(value, "dp", [(0, 1), (1, 0)])


def exchange(value, experts):
    rows, features = value.shape
    parts = value.reshape(experts, rows // experts, features)
    moved = lax.all_to_all(parts, "expert", split_axis=0, concat_axis=0, tiled=True)
    return moved.reshape(rows, features)


def call(kernel, args, outs, limit, grid=(), scratch=(), pinned=False):
    in_specs = [spec for _, spec in args]
    return pl.pallas_call(
        kernel,
        grid=grid,
        in_specs=in_specs,
        out_specs=[spec for _, _, spec in outs],
        out_shape=[(pltpu.HBM if pinned else jax.ShapeDtypeStruct)(shape, kind) for shape, kind, _ in outs],
        scratch_shapes=scratch,
        compiler_params=pltpu.CompilerParams(vmem_limit_bytes=limit * MIB),
        cost_estimate=pl.CostEstimate(flops=1000, bytes_accessed=1000, transcendentals=0),
    )(*[arg for arg, _ in args])


def pin(arg):
    return pltpu.with_memory_space_constraint(arg, pltpu.HBM)


def whole(arg):
    return arg, pl.BlockSpec(memory_space=pltpu.VMEM)


def fixed(arg):
    return arg, pl.BlockSpec(arg.shape, lambda i: (0, 0))


def across(arg, columns):
    return arg, pl.BlockSpec((arg.shape[0], columns), lambda i: (0, i))


def by_rows(arg, steps):
    return pin(arg), pl.BlockSpec((arg.shape[0] // steps, arg.shape[1]), lambda i: (i, 0))


def out_rows(rows, columns, kind, steps):
    return (rows, columns), kind, pl.BlockSpec((rows // steps, columns), lambda i: (i, 0))


def peer_blocks(peers, steps):
    each = steps // PARTS
    blocks = []
    for part, peer in enumerate(peers):
        index = lambda i, part=part: (jnp.clip(i - part * each, 0, each - 1), 0)
        blocks.append((peer, pl.BlockSpec((peer.shape[0] // each, peer.shape[1]), index)))
    return blocks


def by_column(rows, columns, kind, wide):
    return (rows, columns), kind, pl.BlockSpec((rows, wide), lambda i: (0, i))


def joined(refs):
    return jnp.concatenate([ref[...] for ref in refs], axis=0)


def hidden_parts(rows, gate_matrix, up_matrix):
    gate_pre = dot(rows, gate_matrix, ((1,), (0,)))
    up_pre = dot(rows, up_matrix, ((1,), (0,)))
    sig_gate = jax.nn.sigmoid(gate_pre)
    activated = gate_pre * sig_gate
    hidden = (activated * up_pre).astype(BF16)
    gate_slope = up_pre * sig_gate * (1.0 + gate_pre * (1.0 - sig_gate))
    return hidden, activated, gate_slope


def grad_parts(grads, act, slope, down_matrix):
    hidden_grad = dot(grads, down_matrix, ((1,), (1,)))
    return (hidden_grad * slope).astype(BF16), (hidden_grad * act).astype(BF16)


def input_parts(gate_grad, up_grad, gate_matrix, up_matrix):
    return dot(gate_grad, gate_matrix, ((1,), (1,))) + dot(up_grad, up_matrix, ((1,), (1,)))


def places(routing_ref, position_ref, experts, capacity):
    top_count, tok_rows = routing_ref.shape
    expert_ids = lax.broadcasted_iota(jnp.int32, (experts, tok_rows), 0)
    named = [routing_ref[column : column + 1] == expert_ids for column in range(top_count)]
    counts = sum(hit.astype(F32) for hit in named)
    earlier = lax.broadcasted_iota(jnp.int32, (tok_rows, tok_rows), 0) < lax.broadcasted_iota(
        jnp.int32, (tok_rows, tok_rows), 1
    )
    before = dot(counts.astype(BF16), earlier.astype(F32).astype(BF16), ((1,), (0,)))
    for column, hit in enumerate(named):
        slot = jnp.sum(jnp.where(hit, before, 0.0), axis=0, keepdims=True).astype(jnp.int32)
        position_ref[column : column + 1] = routing_ref[column : column + 1] * capacity + slot


def dispatch_kernel(
    routing_ref, weight_ref, tokens_ref, cotangent_ref, position_ref, kept_ref, rows_ref, grads_ref, pick_ref, scale_ref, *, experts, capacity
):
    @pl.when(pl.program_id(0) == 0)
    def _():
        places(routing_ref, position_ref, experts, capacity)
        kept_ref[...] = weight_ref[...]
        slots = lax.broadcasted_iota(jnp.int32, pick_ref.shape, 0)
        columns = range(position_ref.shape[0])
        hits = [position_ref[column : column + 1] == slots for column in columns]
        pick_ref[...] = sum(hit.astype(F32) for hit in hits).astype(BF16)
        scale = sum(jnp.where(hits[column], weight_ref[column : column + 1], 0.0) for column in columns)
        scale_ref[...] = jnp.broadcast_to(jnp.sum(scale, axis=1, keepdims=True), scale_ref.shape)

    rows_ref[...] = dot(pick_ref[...], tokens_ref[...], ((1,), (0,))).astype(BF16)
    grads = dot(pick_ref[...], cotangent_ref[...], ((1,), (0,)))
    grads_ref[...] = (scale_ref[:, :1] * grads).astype(BF16)


def combine_kernel(position_ref, weight_ref, out_ref, input_ref, combined_ref, token_grad_ref, pick_ref):
    tok_rows, top_count = position_ref.shape

    @pl.when(pl.program_id(0) == 0)
    def _():
        slots = lax.broadcasted_iota(jnp.int32, (tok_rows, pick_ref.shape[1]), 1)
        picks = [(position_ref[:, column : column + 1] == slots).astype(F32) for column in range(top_count)]
        for column, pick in enumerate(picks + [sum(picks)]):
            pick_ref[column * tok_rows : (column + 1) * tok_rows] = pick.astype(BF16)

    found = dot(pick_ref[: top_count * tok_rows], out_ref[...], ((1,), (0,)))
    total = jnp.zeros(combined_ref.shape, F32)
    for column in range(top_count):
        total += weight_ref[:, column : column + 1] * found[column * tok_rows : (column + 1) * tok_rows]
    combined_ref[...] = total.astype(BF16)
    token_grad_ref[...] = dot(pick_ref[top_count * tok_rows :], input_ref[...], ((1,), (0,))).astype(BF16)


def hidden_kernel(rows_ref, gate_ref, up_ref, hidden_ref, act_ref, slope_ref):
    hidden_ref[...], act_ref[...], slope_ref[...] = hidden_parts(rows_ref[...], gate_ref[...], up_ref[...])


def forward_kernel(rows_ref, gate_ref, up_ref, down_ref, hidden_ref, act_ref, slope_ref, *out_refs):
    hidden, act_ref[...], slope_ref[...] = hidden_parts(rows_ref[...], gate_ref[...], up_ref[...])
    hidden_ref[...] = hidden
    out = dot(hidden, down_ref[...], ((1,), (0,))).astype(BF16)
    for i, out_ref in enumerate(out_refs):

        @pl.when(pl.program_id(0) == i)
        def _():
            out_ref[...] = out


def peer_part(peer_refs):
    return jnp.where(pl.program_id(0) < pl.num_programs(0) // PARTS, peer_refs[0][...], peer_refs[1][...]).astype(F32)


def out_kernel(hidden_ref, down_ref, *refs):
    out_ref = refs[-1]
    total = dot(hidden_ref[...], down_ref[...], ((1,), (0,)))
    out_ref[...] = (total + peer_part(refs[:-1])).astype(BF16)


def grad_kernel(grads_ref, act_ref, slope_ref, down_ref, gate_grad_ref, up_grad_ref):
    gate_grad_ref[...], up_grad_ref[...] = grad_parts(grads_ref[...], act_ref[...], slope_ref[...], down_ref[...])


def backward_kernel(grads_ref, act_ref, slope_ref, gate_ref, up_ref, down_ref, gate_grad_ref, up_grad_ref, *in_refs):
    gate_grad, up_grad = grad_parts(grads_ref[...], act_ref[...], slope_ref[...], down_ref[...])
    gate_grad_ref[...] = gate_grad
    up_grad_ref[...] = up_grad
    back = input_parts(gate_grad, up_grad, gate_ref[...], up_ref[...]).astype(BF16)
    for i, in_ref in enumerate(in_refs):

        @pl.when(pl.program_id(0) == i)
        def _():
            in_ref[...] = back


def input_kernel(gate_grad_ref, up_grad_ref, gate_ref, up_ref, *refs):
    out_ref = refs[-1]
    total = input_parts(gate_grad_ref[...], up_grad_ref[...], gate_ref[...], up_ref[...])
    out_ref[...] = (total + peer_part(refs[:-1])).astype(BF16)


def weight_kernel(*refs):
    rows, grads, hidden, gate_grad, up_grad = (refs[2 * i : 2 * i + 2] for i in range(5))
    gate_out, up_out, down_out = refs[10:]
    both = jnp.concatenate([joined(gate_grad), joined(up_grad)], axis=1)
    total = dot(joined(rows), both, ((0,), (0,)))
    width = gate_out.shape[1]
    gate_out[...] = total[:, :width].astype(BF16)
    up_out[...] = total[:, width:].astype(BF16)
    down_out[...] = dot(joined(hidden), joined(grads), ((0,), (0,))).astype(BF16)


def weight_grads(wide, kept):
    features = wide[0].shape[1]
    width = kept[0].shape[1]
    args = [across(pin(value), COLUMNS) for value in wide] + [fixed(pin(value)) for value in kept]
    tall = ((features, width), BF16, pl.BlockSpec((COLUMNS, width), lambda i: (i, 0)))
    return call(weight_kernel, args, [tall, tall, by_column(width, features, BF16, COLUMNS)], 48, grid=(features // COLUMNS,))


def local(tokens, cotangent, routing, combine_weights, w_gate, w_up, w_down):
    tok_rows, features = tokens.shape
    top_count = routing.shape[1]
    experts = lax.axis_size("expert")
    cold_count = experts - HOT
    hot_cap = 2 * tok_rows * top_count // experts
    cold_cap = (tok_rows * top_count - HOT * hot_cap + cold_count - 1) // cold_count
    capacity = max(hot_cap, cold_cap)
    local_rows = experts * capacity
    gate_matrix, up_matrix, down_matrix = w_gate[0], w_up[0], w_down[0]
    width = gate_matrix.shape[1]
    broad_grid = (features // BROAD,)
    place_shape = (top_count, tok_rows)
    sent = by_column(local_rows, features, BF16, BROAD)
    position, route_weights, send_rows, send_grads = call(
        functools.partial(dispatch_kernel, experts=experts, capacity=capacity),
        [fixed(pin(routing.T)), fixed(pin(combine_weights.T)), across(pin(tokens), BROAD), across(pin(cotangent), BROAD)],
        [(place_shape, kind, pl.BlockSpec(place_shape, lambda i: (0, 0))) for kind in (jnp.int32, F32)] + [sent, sent],
        40,
        grid=broad_grid,
        scratch=[pltpu.VMEM((local_rows, tok_rows), BF16), pltpu.VMEM((local_rows, 128), F32)],
        pinned=True,
    )
    rows_own = exchange(send_rows, experts)
    rows_own, send_grads, position, route_weights = lax.optimization_barrier(
        (rows_own, send_grads, position, route_weights)
    )
    position, route_weights = position.T, route_weights.T
    grads_own = exchange(send_grads, experts)

    weights = [whole(matrix) for matrix in (gate_matrix, up_matrix, down_matrix)]
    kept = [out_rows(local_rows, width, kind, PARTS) for kind in (BF16, F32, F32)]
    pair = [out_rows(local_rows, width, BF16, PARTS)] * 2
    part = (local_rows // PARTS, features)
    parts = [(part, BF16, pl.BlockSpec(part, lambda i: (0, 0)))] * PARTS
    send = [out_rows(local_rows, features, BF16, STEPS)]
    halves = dict(grid=(PARTS,), pinned=True)
    steps = dict(grid=(STEPS,), pinned=True)

    rows_peer = swap(rows_own)
    hidden_own, act_own, slope_own = call(hidden_kernel, [by_rows(rows_own, PARTS)] + weights[:2], kept, 32, **halves)
    hidden_peer, act_peer, slope_peer, *outs = call(
        forward_kernel, [by_rows(rows_peer, PARTS)] + weights, kept + parts, 44, **halves
    )
    outs = [swap(out) for out in outs]
    (out_send,) = call(
        out_kernel, [by_rows(hidden_own, STEPS)] + weights[2:] + peer_blocks(outs, STEPS), send, 32, **steps
    )
    grads_own, out_send = lax.optimization_barrier((grads_own, out_send))
    out_back = exchange(out_send, experts)

    grads_peer = swap(grads_own)
    gate_own, up_own = call(
        grad_kernel,
        [by_rows(value, PARTS) for value in (grads_own, act_own, slope_own)] + weights[2:],
        pair,
        32,
        **halves,
    )
    gate_peer, up_peer, *ins = call(
        backward_kernel,
        [by_rows(value, PARTS) for value in (grads_peer, act_peer, slope_peer)] + weights,
        pair + parts,
        44,
        **halves,
    )
    ins = [swap(value) for value in ins]
    (input_send,) = call(
        input_kernel,
        [by_rows(gate_own, STEPS), by_rows(up_own, STEPS)] + weights[:2] + peer_blocks(ins, STEPS),
        send,
        32,
        **steps,
    )
    wgrads = weight_grads(
        [rows_own, rows_peer, grads_own, grads_peer],
        [hidden_own, hidden_peer, gate_own, gate_peer, up_own, up_peer],
    )
    out_back, input_send, position, route_weights, *wgrads = lax.optimization_barrier(
        (out_back, input_send, position, route_weights, *wgrads)
    )
    input_back = exchange(input_send, experts)
    combined, token_grad = call(
        combine_kernel,
        [fixed(position), fixed(route_weights), across(out_back, BROAD), across(input_back, BROAD)],
        [by_column(tok_rows, features, BF16, BROAD)] * 2,
        40,
        grid=broad_grid,
        scratch=[pltpu.VMEM(((top_count + 1) * tok_rows, local_rows), BF16)],
    )
    return combined, token_grad, wgrads[0][None], wgrads[1][None], wgrads[2][None]


def solution(mesh):
    in_specs = (
        P(("dp", "expert"), None),
        P(("dp", "expert"), None),
        P(("dp", "expert"), None),
        P(("dp", "expert"), None),
        P("expert", None, "dp"),
        P("expert", None, "dp"),
        P("expert", "dp", None),
    )
    out_specs = (
        P(("dp", "expert"), None),
        P(("dp", "expert"), None),
        P("expert", None, "dp"),
        P("expert", None, "dp"),
        P("expert", "dp", None),
    )
    return jax.shard_map(local, mesh=mesh, in_specs=in_specs, out_specs=out_specs, check_vma=False)
```

```python
import functools

import jax
import jax.numpy as jnp
from jax import lax
from jax.experimental import pallas as pl
from jax.experimental.pallas import tpu as pltpu
from jax.sharding import PartitionSpec as P

HOT = 4
COLUMNS = 1024
BROAD = 2048
PARTS = 2
STEPS = 2
BF16 = jnp.bfloat16
F32 = jnp.float32
MIB = 1024 * 1024


def dot(left, right, dims):
    return lax.dot_general(left, right, (dims, ((), ())), preferred_element_type=F32)


def swap(value):
    return lax.ppermute(value, "dp", [(0, 1), (1, 0)])


def exchange(value, experts):
    rows, features = value.shape
    parts = value.reshape(experts, rows // experts, features)
    moved = lax.all_to_all(parts, "expert", split_axis=0, concat_axis=0, tiled=True)
    return moved.reshape(rows, features)


def call(kernel, args, outs, limit, grid=(), scratch=(), pinned=False):
    in_specs = [spec for _, spec in args]
    return pl.pallas_call(
        kernel,
        grid=grid,
        in_specs=in_specs,
        out_specs=[spec for _, _, spec in outs],
        out_shape=[(pltpu.HBM if pinned else jax.ShapeDtypeStruct)(shape, kind) for shape, kind, _ in outs],
        scratch_shapes=scratch,
        compiler_params=pltpu.CompilerParams(vmem_limit_bytes=limit * MIB),
        cost_estimate=pl.CostEstimate(flops=1000, bytes_accessed=1000, transcendentals=0),
    )(*[arg for arg, _ in args])


def pin(arg):
    return pltpu.with_memory_space_constraint(arg, pltpu.HBM)


def whole(arg):
    return arg, pl.BlockSpec(memory_space=pltpu.VMEM)


def resident(arg):
    return pin(arg), pl.BlockSpec(arg.shape, lambda i: (0, 0), pipeline_mode=pl.Buffered(1))


def fixed(arg):
    return arg, pl.BlockSpec(arg.shape, lambda i: (0, 0))


def across(arg, columns):
    return arg, pl.BlockSpec((arg.shape[0], columns), lambda i: (0, i))


def by_rows(arg, steps):
    return pin(arg), pl.BlockSpec((arg.shape[0] // steps, arg.shape[1]), lambda i: (i, 0))


def out_rows(rows, columns, kind, steps):
    return (rows, columns), kind, pl.BlockSpec((rows // steps, columns), lambda i: (i, 0))


def peer_blocks(peers, steps):
    each = steps // PARTS
    blocks = []
    for part, peer in enumerate(peers):
        index = lambda i, part=part: (jnp.clip(i - part * each, 0, each - 1), 0)
        blocks.append((peer, pl.BlockSpec((peer.shape[0] // each, peer.shape[1]), index)))
    return blocks


def by_column(rows, columns, kind, wide):
    return (rows, columns), kind, pl.BlockSpec((rows, wide), lambda i: (0, i))


def joined(refs):
    return jnp.concatenate([ref[...] for ref in refs], axis=0)


def hidden_parts(rows, gate_matrix, up_matrix):
    gate_pre = dot(rows, gate_matrix, ((1,), (0,)))
    up_pre = dot(rows, up_matrix, ((1,), (0,)))
    sig_gate = jax.nn.sigmoid(gate_pre)
    activated = gate_pre * sig_gate
    hidden = (activated * up_pre).astype(BF16)
    gate_slope = up_pre * sig_gate * (1.0 + gate_pre * (1.0 - sig_gate))
    return hidden, activated, gate_slope


def grad_parts(grads, act, slope, down_matrix):
    hidden_grad = dot(grads, down_matrix, ((1,), (1,)))
    return (hidden_grad * slope).astype(BF16), (hidden_grad * act).astype(BF16)


def input_parts(gate_grad, up_grad, gate_matrix, up_matrix):
    return dot(gate_grad, gate_matrix, ((1,), (1,))) + dot(up_grad, up_matrix, ((1,), (1,)))


def places(routing_ref, position_ref, experts, capacity):
    top_count, tok_rows = routing_ref.shape
    expert_ids = lax.broadcasted_iota(jnp.int32, (experts, tok_rows), 0)
    named = [routing_ref[column : column + 1] == expert_ids for column in range(top_count)]
    counts = sum(hit.astype(F32) for hit in named)
    earlier = lax.broadcasted_iota(jnp.int32, (tok_rows, tok_rows), 0) < lax.broadcasted_iota(
        jnp.int32, (tok_rows, tok_rows), 1
    )
    before = dot(counts.astype(BF16), earlier.astype(F32).astype(BF16), ((1,), (0,)))
    for column, hit in enumerate(named):
        slot = jnp.sum(jnp.where(hit, before, 0.0), axis=0, keepdims=True).astype(jnp.int32)
        position_ref[column : column + 1] = routing_ref[column : column + 1] * capacity + slot


def dispatch_kernel(
    routing_ref, weight_ref, tokens_ref, cotangent_ref, position_ref, kept_ref, rows_ref, grads_ref, pick_ref, scale_ref, *, experts, capacity
):
    @pl.when(pl.program_id(0) == 0)
    def _():
        places(routing_ref, position_ref, experts, capacity)
        kept_ref[...] = weight_ref[...]
        slots = lax.broadcasted_iota(jnp.int32, pick_ref.shape, 0)
        columns = range(position_ref.shape[0])
        hits = [position_ref[column : column + 1] == slots for column in columns]
        pick_ref[...] = sum(hit.astype(F32) for hit in hits).astype(BF16)
        scale = sum(jnp.where(hits[column], weight_ref[column : column + 1], 0.0) for column in columns)
        scale_ref[...] = jnp.broadcast_to(jnp.sum(scale, axis=1, keepdims=True), scale_ref.shape)

    rows_ref[...] = dot(pick_ref[...], tokens_ref[...], ((1,), (0,))).astype(BF16)
    grads = dot(pick_ref[...], cotangent_ref[...], ((1,), (0,)))
    grads_ref[...] = (scale_ref[:, :1] * grads).astype(BF16)


def combine_kernel(position_ref, weight_ref, out_ref, input_ref, combined_ref, token_grad_ref, pick_ref):
    tok_rows, top_count = position_ref.shape

    @pl.when(pl.program_id(0) == 0)
    def _():
        slots = lax.broadcasted_iota(jnp.int32, (tok_rows, pick_ref.shape[1]), 1)
        picks = [(position_ref[:, column : column + 1] == slots).astype(F32) for column in range(top_count)]
        for column, pick in enumerate(picks + [sum(picks)]):
            pick_ref[column * tok_rows : (column + 1) * tok_rows] = pick.astype(BF16)

    found = dot(pick_ref[: top_count * tok_rows], out_ref[...], ((1,), (0,)))
    total = jnp.zeros(combined_ref.shape, F32)
    for column in range(top_count):
        total += weight_ref[:, column : column + 1] * found[column * tok_rows : (column + 1) * tok_rows]
    combined_ref[...] = total.astype(BF16)
    token_grad_ref[...] = dot(pick_ref[top_count * tok_rows :], input_ref[...], ((1,), (0,))).astype(BF16)


def hidden_kernel(rows_ref, gate_ref, up_ref, hidden_ref, act_ref, slope_ref):
    hidden_ref[...], act_ref[...], slope_ref[...] = hidden_parts(rows_ref[...], gate_ref[...], up_ref[...])


def forward_kernel(rows_ref, gate_ref, up_ref, down_ref, hidden_ref, act_ref, slope_ref, *out_refs):
    hidden, act_ref[...], slope_ref[...] = hidden_parts(rows_ref[...], gate_ref[...], up_ref[...])
    hidden_ref[...] = hidden
    out = dot(hidden, down_ref[...], ((1,), (0,))).astype(BF16)
    for i, out_ref in enumerate(out_refs):

        @pl.when(pl.program_id(0) == i)
        def _():
            out_ref[...] = out


def peer_part(peer_refs):
    return jnp.where(pl.program_id(0) < pl.num_programs(0) // PARTS, peer_refs[0][...], peer_refs[1][...]).astype(F32)


def out_kernel(hidden_ref, down_ref, *refs):
    out_ref = refs[-1]
    total = dot(hidden_ref[...], down_ref[...], ((1,), (0,)))
    out_ref[...] = (total + peer_part(refs[:-1])).astype(BF16)


def grad_kernel(grads_ref, act_ref, slope_ref, down_ref, gate_grad_ref, up_grad_ref):
    gate_grad_ref[...], up_grad_ref[...] = grad_parts(grads_ref[...], act_ref[...], slope_ref[...], down_ref[...])


def backward_kernel(grads_ref, act_ref, slope_ref, gate_ref, up_ref, down_ref, gate_grad_ref, up_grad_ref, *in_refs):
    gate_grad, up_grad = grad_parts(grads_ref[...], act_ref[...], slope_ref[...], down_ref[...])
    gate_grad_ref[...] = gate_grad
    up_grad_ref[...] = up_grad
    back = input_parts(gate_grad, up_grad, gate_ref[...], up_ref[...]).astype(BF16)
    for i, in_ref in enumerate(in_refs):

        @pl.when(pl.program_id(0) == i)
        def _():
            in_ref[...] = back


def input_kernel(gate_grad_ref, up_grad_ref, gate_ref, up_ref, *refs):
    out_ref = refs[-1]
    total = input_parts(gate_grad_ref[...], up_grad_ref[...], gate_ref[...], up_ref[...])
    out_ref[...] = (total + peer_part(refs[:-1])).astype(BF16)


def weight_kernel(*refs):
    rows, grads, hidden, gate_grad, up_grad = (refs[2 * i : 2 * i + 2] for i in range(5))
    gate_out, up_out, down_out = refs[10:]
    both = jnp.concatenate([joined(gate_grad), joined(up_grad)], axis=1)
    total = dot(joined(rows), both, ((0,), (0,)))
    width = gate_out.shape[1]
    gate_out[...] = total[:, :width].astype(BF16)
    up_out[...] = total[:, width:].astype(BF16)
    down_out[...] = dot(joined(hidden), joined(grads), ((0,), (0,))).astype(BF16)


def weight_grads(wide, kept):
    features = wide[0].shape[1]
    width = kept[0].shape[1]
    args = [across(pin(value), COLUMNS) for value in wide] + [fixed(pin(value)) for value in kept]
    tall = ((features, width), BF16, pl.BlockSpec((COLUMNS, width), lambda i: (i, 0)))
    return call(weight_kernel, args, [tall, tall, by_column(width, features, BF16, COLUMNS)], 48, grid=(features // COLUMNS,))


def local(tokens, cotangent, routing, combine_weights, w_gate, w_up, w_down):
    tok_rows, features = tokens.shape
    top_count = routing.shape[1]
    experts = lax.axis_size("expert")
    cold_count = experts - HOT
    hot_cap = 2 * tok_rows * top_count // experts
    cold_cap = (tok_rows * top_count - HOT * hot_cap + cold_count - 1) // cold_count
    capacity = max(hot_cap, cold_cap)
    local_rows = experts * capacity
    gate_matrix, up_matrix, down_matrix = w_gate[0], w_up[0], w_down[0]
    width = gate_matrix.shape[1]
    broad_grid = (features // BROAD,)
    place_shape = (top_count, tok_rows)
    sent = by_column(local_rows, features, BF16, BROAD)
    position, route_weights, send_rows, send_grads = call(
        functools.partial(dispatch_kernel, experts=experts, capacity=capacity),
        [fixed(pin(routing.T)), fixed(pin(combine_weights.T)), across(pin(tokens), BROAD), across(pin(cotangent), BROAD)],
        [(place_shape, kind, pl.BlockSpec(place_shape, lambda i: (0, 0))) for kind in (jnp.int32, F32)] + [sent, sent],
        40,
        grid=broad_grid,
        scratch=[pltpu.VMEM((local_rows, tok_rows), BF16), pltpu.VMEM((local_rows, 128), F32)],
        pinned=True,
    )
    rows_own = exchange(send_rows, experts)
    rows_own, send_grads, position, route_weights = lax.optimization_barrier(
        (rows_own, send_grads, position, route_weights)
    )
    position, route_weights = position.T, route_weights.T
    grads_own = exchange(send_grads, experts)

    weights = [whole(matrix) for matrix in (gate_matrix, up_matrix, down_matrix)]
    own_weights = [resident(matrix) for matrix in (gate_matrix, up_matrix, down_matrix)]
    kept = [out_rows(local_rows, width, kind, PARTS) for kind in (BF16, F32, F32)]
    pair = [out_rows(local_rows, width, BF16, PARTS)] * 2
    part = (local_rows // PARTS, features)
    parts = [(part, BF16, pl.BlockSpec(part, lambda i: (0, 0)))] * PARTS
    send = [out_rows(local_rows, features, BF16, STEPS)]
    halves = dict(grid=(PARTS,), pinned=True)
    steps = dict(grid=(STEPS,), pinned=True)

    rows_peer = swap(rows_own)
    hidden_own, act_own, slope_own = call(hidden_kernel, [by_rows(rows_own, PARTS)] + weights[:2], kept, 32, **halves)
    hidden_peer, act_peer, slope_peer, *outs = call(
        forward_kernel, [by_rows(rows_peer, PARTS)] + weights, kept + parts, 44, **halves
    )
    outs = [swap(out) for out in outs]
    (out_send,) = call(
        out_kernel, [by_rows(hidden_own, STEPS)] + weights[2:] + peer_blocks(outs, STEPS), send, 32, **steps
    )
    grads_own, out_send = lax.optimization_barrier((grads_own, out_send))
    out_back = exchange(out_send, experts)

    grads_peer = swap(grads_own)
    gate_own, up_own = call(
        grad_kernel,
        [by_rows(value, PARTS) for value in (grads_own, act_own, slope_own)] + weights[2:],
        pair,
        32,
        **halves,
    )
    gate_peer, up_peer, *ins = call(
        backward_kernel,
        [by_rows(value, PARTS) for value in (grads_peer, act_peer, slope_peer)] + own_weights,
        pair + parts,
        44,
        **halves,
    )
    ins = [swap(value) for value in ins]
    (input_send,) = call(
        input_kernel,
        [by_rows(gate_own, STEPS), by_rows(up_own, STEPS)] + weights[:2] + peer_blocks(ins, STEPS),
        send,
        32,
        **steps,
    )
    wgrads = weight_grads(
        [rows_own, rows_peer, grads_own, grads_peer],
        [hidden_own, hidden_peer, gate_own, gate_peer, up_own, up_peer],
    )
    out_back, input_send, position, route_weights, *wgrads = lax.optimization_barrier(
        (out_back, input_send, position, route_weights, *wgrads)
    )
    input_back = exchange(input_send, experts)
    combined, token_grad = call(
        combine_kernel,
        [fixed(position), fixed(route_weights), across(out_back, BROAD), across(input_back, BROAD)],
        [by_column(tok_rows, features, BF16, BROAD)] * 2,
        40,
        grid=broad_grid,
        scratch=[pltpu.VMEM(((top_count + 1) * tok_rows, local_rows), BF16)],
    )
    return combined, token_grad, wgrads[0][None], wgrads[1][None], wgrads[2][None]


def solution(mesh):
    in_specs = (
        P(("dp", "expert"), None),
        P(("dp", "expert"), None),
        P(("dp", "expert"), None),
        P(("dp", "expert"), None),
        P("expert", None, "dp"),
        P("expert", None, "dp"),
        P("expert", "dp", None),
    )
    out_specs = (
        P(("dp", "expert"), None),
        P(("dp", "expert"), None),
        P("expert", None, "dp"),
        P("expert", None, "dp"),
        P("expert", "dp", None),
    )
    return jax.shard_map(local, mesh=mesh, in_specs=in_specs, out_specs=out_specs, check_vma=False)
```

```python
import functools

import jax
import jax.numpy as jnp
from jax import lax
from jax.experimental import pallas as pl
from jax.experimental.pallas import tpu as pltpu
from jax.sharding import PartitionSpec as P

HOT = 4
COLUMNS = 1024
BROAD = 2048
PARTS = 2
STEPS = 2
BF16 = jnp.bfloat16
F32 = jnp.float32
MIB = 1024 * 1024


def dot(left, right, dims):
    return lax.dot_general(left, right, (dims, ((), ())), preferred_element_type=F32)


def swap(value):
    return lax.ppermute(value, "dp", [(0, 1), (1, 0)])


def exchange(value, experts):
    rows, features = value.shape
    parts = value.reshape(experts, rows // experts, features)
    moved = lax.all_to_all(parts, "expert", split_axis=0, concat_axis=0, tiled=True)
    return moved.reshape(rows, features)


def call(kernel, args, outs, limit, grid=(), scratch=(), pinned=False):
    in_specs = [spec for _, spec in args]
    return pl.pallas_call(
        kernel,
        grid=grid,
        in_specs=in_specs,
        out_specs=[spec for _, _, spec in outs],
        out_shape=[
            (pltpu.HBM if pinned and spec.memory_space is None else jax.ShapeDtypeStruct)(shape, kind)
            for shape, kind, spec in outs
        ],
        scratch_shapes=scratch,
        compiler_params=pltpu.CompilerParams(vmem_limit_bytes=limit * MIB),
        cost_estimate=pl.CostEstimate(flops=1000, bytes_accessed=1000, transcendentals=0),
    )(*[arg for arg, _ in args])


def pin(arg):
    return pltpu.with_memory_space_constraint(arg, pltpu.HBM)


def whole(arg):
    return arg, pl.BlockSpec(memory_space=pltpu.VMEM)


def resident(arg):
    return pin(arg), pl.BlockSpec(arg.shape, lambda i: (0, 0), pipeline_mode=pl.Buffered(1))


def fixed(arg):
    return arg, pl.BlockSpec(arg.shape, lambda i: (0, 0))


def across(arg, columns):
    return arg, pl.BlockSpec((arg.shape[0], columns), lambda i: (0, i))


def by_rows(arg, steps):
    return pin(arg), pl.BlockSpec((arg.shape[0] // steps, arg.shape[1]), lambda i: (i, 0))


def out_rows(rows, columns, kind, steps):
    return (rows, columns), kind, pl.BlockSpec((rows // steps, columns), lambda i: (i, 0))


def peer_blocks(peers, steps):
    each = steps // PARTS
    blocks = []
    for part, peer in enumerate(peers):
        index = lambda i, part=part: (jnp.clip(i - part * each, 0, each - 1), 0)
        blocks.append((peer, pl.BlockSpec((peer.shape[0] // each, peer.shape[1]), index)))
    return blocks


def by_column(rows, columns, kind, wide):
    return (rows, columns), kind, pl.BlockSpec((rows, wide), lambda i: (0, i))


def joined(refs):
    return jnp.concatenate([ref[...] for ref in refs], axis=0)


def hidden_parts(rows, gate_matrix, up_matrix):
    gate_pre = dot(rows, gate_matrix, ((1,), (0,)))
    up_pre = dot(rows, up_matrix, ((1,), (0,)))
    sig_gate = jax.nn.sigmoid(gate_pre)
    activated = gate_pre * sig_gate
    hidden = (activated * up_pre).astype(BF16)
    gate_slope = up_pre * sig_gate * (1.0 + gate_pre * (1.0 - sig_gate))
    return hidden, activated, gate_slope


def grad_parts(grads, act, slope, down_matrix):
    hidden_grad = dot(grads, down_matrix, ((1,), (1,)))
    return (hidden_grad * slope).astype(BF16), (hidden_grad * act).astype(BF16)


def input_parts(gate_grad, up_grad, gate_matrix, up_matrix):
    return dot(gate_grad, gate_matrix, ((1,), (1,))) + dot(up_grad, up_matrix, ((1,), (1,)))


def places(routing_ref, position_ref, experts, capacity):
    top_count, tok_rows = routing_ref.shape
    expert_ids = lax.broadcasted_iota(jnp.int32, (experts, tok_rows), 0)
    named = [routing_ref[column : column + 1] == expert_ids for column in range(top_count)]
    counts = sum(hit.astype(F32) for hit in named)
    earlier = lax.broadcasted_iota(jnp.int32, (tok_rows, tok_rows), 0) < lax.broadcasted_iota(
        jnp.int32, (tok_rows, tok_rows), 1
    )
    before = dot(counts.astype(BF16), earlier.astype(F32).astype(BF16), ((1,), (0,)))
    for column, hit in enumerate(named):
        slot = jnp.sum(jnp.where(hit, before, 0.0), axis=0, keepdims=True).astype(jnp.int32)
        position_ref[column : column + 1] = routing_ref[column : column + 1] * capacity + slot


def dispatch_kernel(
    routing_ref, weight_ref, tokens_ref, cotangent_ref, position_ref, kept_ref, rows_ref, grads_ref, pick_ref, scale_ref, *, experts, capacity
):
    @pl.when(pl.program_id(0) == 0)
    def _():
        places(routing_ref, position_ref, experts, capacity)
        kept_ref[...] = weight_ref[...]
        slots = lax.broadcasted_iota(jnp.int32, pick_ref.shape, 0)
        columns = range(position_ref.shape[0])
        hits = [position_ref[column : column + 1] == slots for column in columns]
        pick_ref[...] = sum(hit.astype(F32) for hit in hits).astype(BF16)
        scale = sum(jnp.where(hits[column], weight_ref[column : column + 1], 0.0) for column in columns)
        scale_ref[...] = jnp.broadcast_to(jnp.sum(scale, axis=1, keepdims=True), scale_ref.shape)

    columns = tokens_ref.shape[1]
    here = pl.ds(pl.multiple_of(pl.program_id(0) * columns, columns), columns)
    rows_ref[:, here] = dot(pick_ref[...], tokens_ref[...], ((1,), (0,))).astype(BF16)
    grads = dot(pick_ref[...], cotangent_ref[...], ((1,), (0,)))
    grads_ref[...] = (scale_ref[:, :1] * grads).astype(BF16)


def combine_kernel(position_ref, weight_ref, out_ref, input_ref, combined_ref, token_grad_ref, pick_ref):
    tok_rows, top_count = position_ref.shape

    @pl.when(pl.program_id(0) == 0)
    def _():
        slots = lax.broadcasted_iota(jnp.int32, (tok_rows, pick_ref.shape[1]), 1)
        picks = [(position_ref[:, column : column + 1] == slots).astype(F32) for column in range(top_count)]
        for column, pick in enumerate(picks + [sum(picks)]):
            pick_ref[column * tok_rows : (column + 1) * tok_rows] = pick.astype(BF16)

    found = dot(pick_ref[: top_count * tok_rows], out_ref[...], ((1,), (0,)))
    total = jnp.zeros(combined_ref.shape, F32)
    for column in range(top_count):
        total += weight_ref[:, column : column + 1] * found[column * tok_rows : (column + 1) * tok_rows]
    combined_ref[...] = total.astype(BF16)
    token_grad_ref[...] = dot(pick_ref[top_count * tok_rows :], input_ref[...], ((1,), (0,))).astype(BF16)


def hidden_kernel(rows_ref, gate_ref, up_ref, hidden_ref, act_ref, slope_ref):
    hidden_ref[...], act_ref[...], slope_ref[...] = hidden_parts(rows_ref[...], gate_ref[...], up_ref[...])


def forward_kernel(rows_ref, gate_ref, up_ref, down_ref, hidden_ref, act_ref, slope_ref, *out_refs):
    hidden, act_ref[...], slope_ref[...] = hidden_parts(rows_ref[...], gate_ref[...], up_ref[...])
    hidden_ref[...] = hidden
    out = dot(hidden, down_ref[...], ((1,), (0,))).astype(BF16)
    for i, out_ref in enumerate(out_refs):

        @pl.when(pl.program_id(0) == i)
        def _():
            out_ref[...] = out


def peer_part(peer_refs):
    return jnp.where(pl.program_id(0) < pl.num_programs(0) // PARTS, peer_refs[0][...], peer_refs[1][...]).astype(F32)


def out_kernel(hidden_ref, down_ref, *refs):
    out_ref = refs[-1]
    total = dot(hidden_ref[...], down_ref[...], ((1,), (0,)))
    out_ref[...] = (total + peer_part(refs[:-1])).astype(BF16)


def grad_kernel(grads_ref, act_ref, slope_ref, down_ref, gate_grad_ref, up_grad_ref):
    gate_grad_ref[...], up_grad_ref[...] = grad_parts(grads_ref[...], act_ref[...], slope_ref[...], down_ref[...])


def backward_kernel(grads_ref, act_ref, slope_ref, gate_ref, up_ref, down_ref, gate_grad_ref, up_grad_ref, *in_refs):
    gate_grad, up_grad = grad_parts(grads_ref[...], act_ref[...], slope_ref[...], down_ref[...])
    gate_grad_ref[...] = gate_grad
    up_grad_ref[...] = up_grad
    back = input_parts(gate_grad, up_grad, gate_ref[...], up_ref[...]).astype(BF16)
    for i, in_ref in enumerate(in_refs):

        @pl.when(pl.program_id(0) == i)
        def _():
            in_ref[...] = back


def input_kernel(gate_grad_ref, up_grad_ref, gate_ref, up_ref, *refs):
    out_ref = refs[-1]
    total = input_parts(gate_grad_ref[...], up_grad_ref[...], gate_ref[...], up_ref[...])
    out_ref[...] = (total + peer_part(refs[:-1])).astype(BF16)


def weight_kernel(*refs):
    rows, grads, hidden, gate_grad, up_grad = (refs[2 * i : 2 * i + 2] for i in range(5))
    gate_out, up_out, down_out = refs[10:]
    both = jnp.concatenate([joined(gate_grad), joined(up_grad)], axis=1)
    total = dot(joined(rows), both, ((0,), (0,)))
    width = gate_out.shape[1]
    gate_out[...] = total[:, :width].astype(BF16)
    up_out[...] = total[:, width:].astype(BF16)
    down_out[...] = dot(joined(hidden), joined(grads), ((0,), (0,))).astype(BF16)


def weight_grads(wide, kept):
    features = wide[0].shape[1]
    width = kept[0].shape[1]
    args = [across(pin(value), COLUMNS) for value in wide] + [fixed(pin(value)) for value in kept]
    tall = ((features, width), BF16, pl.BlockSpec((COLUMNS, width), lambda i: (i, 0)))
    return call(weight_kernel, args, [tall, tall, by_column(width, features, BF16, COLUMNS)], 48, grid=(features // COLUMNS,))


def local(tokens, cotangent, routing, combine_weights, w_gate, w_up, w_down):
    tok_rows, features = tokens.shape
    top_count = routing.shape[1]
    experts = lax.axis_size("expert")
    cold_count = experts - HOT
    hot_cap = 2 * tok_rows * top_count // experts
    cold_cap = (tok_rows * top_count - HOT * hot_cap + cold_count - 1) // cold_count
    capacity = max(hot_cap, cold_cap)
    local_rows = experts * capacity
    gate_matrix, up_matrix, down_matrix = w_gate[0], w_up[0], w_down[0]
    width = gate_matrix.shape[1]
    broad_grid = (features // BROAD,)
    place_shape = (top_count, tok_rows)
    sent = by_column(local_rows, features, BF16, BROAD)
    position, route_weights, send_rows, send_grads = call(
        functools.partial(dispatch_kernel, experts=experts, capacity=capacity),
        [fixed(pin(routing.T)), fixed(pin(combine_weights.T)), across(pin(tokens), BROAD), across(pin(cotangent), BROAD)],
        [(place_shape, kind, pl.BlockSpec(place_shape, lambda i: (0, 0))) for kind in (jnp.int32, F32)] + [((local_rows, features), BF16, pl.BlockSpec(memory_space=pltpu.VMEM)), sent],
        40,
        grid=broad_grid,
        scratch=[pltpu.VMEM((local_rows, tok_rows), BF16), pltpu.VMEM((local_rows, 128), F32)],
        pinned=True,
    )
    rows_own = exchange(send_rows, experts)
    rows_own, send_grads, position, route_weights = lax.optimization_barrier(
        (rows_own, send_grads, position, route_weights)
    )
    position, route_weights = position.T, route_weights.T
    grads_own = exchange(send_grads, experts)

    weights = [whole(matrix) for matrix in (gate_matrix, up_matrix, down_matrix)]
    own_weights = [resident(matrix) for matrix in (gate_matrix, up_matrix, down_matrix)]
    kept = [out_rows(local_rows, width, kind, PARTS) for kind in (BF16, F32, F32)]
    pair = [out_rows(local_rows, width, BF16, PARTS)] * 2
    part = (local_rows // PARTS, features)
    parts = [(part, BF16, pl.BlockSpec(part, lambda i: (0, 0)))] * PARTS
    send = [out_rows(local_rows, features, BF16, STEPS)]
    halves = dict(grid=(PARTS,), pinned=True)
    steps = dict(grid=(STEPS,), pinned=True)

    rows_peer = swap(rows_own)
    hidden_own, act_own, slope_own = call(hidden_kernel, [by_rows(rows_own, PARTS)] + weights[:2], kept, 32, **halves)
    hidden_peer, act_peer, slope_peer, *outs = call(
        forward_kernel, [by_rows(rows_peer, PARTS)] + weights, kept + parts, 44, **halves
    )
    outs = [swap(out) for out in outs]
    (out_send,) = call(
        out_kernel, [by_rows(hidden_own, STEPS)] + weights[2:] + peer_blocks(outs, STEPS), send, 32, **steps
    )
    grads_own, out_send = lax.optimization_barrier((grads_own, out_send))
    out_back = exchange(out_send, experts)

    grads_peer = swap(grads_own)
    gate_own, up_own = call(
        grad_kernel,
        [by_rows(value, PARTS) for value in (grads_own, act_own, slope_own)] + weights[2:],
        pair,
        32,
        **halves,
    )
    gate_peer, up_peer, *ins = call(
        backward_kernel,
        [by_rows(value, PARTS) for value in (grads_peer, act_peer, slope_peer)] + own_weights,
        pair + parts,
        44,
        **halves,
    )
    ins = [swap(value) for value in ins]
    (input_send,) = call(
        input_kernel,
        [by_rows(gate_own, STEPS), by_rows(up_own, STEPS)] + weights[:2] + peer_blocks(ins, STEPS),
        send,
        32,
        **steps,
    )
    wgrads = weight_grads(
        [rows_own, rows_peer, grads_own, grads_peer],
        [hidden_own, hidden_peer, gate_own, gate_peer, up_own, up_peer],
    )
    out_back, input_send, position, route_weights, *wgrads = lax.optimization_barrier(
        (out_back, input_send, position, route_weights, *wgrads)
    )
    input_back = exchange(input_send, experts)
    combined, token_grad = call(
        combine_kernel,
        [fixed(position), fixed(route_weights), across(out_back, BROAD), across(input_back, BROAD)],
        [by_column(tok_rows, features, BF16, BROAD)] * 2,
        40,
        grid=broad_grid,
        scratch=[pltpu.VMEM(((top_count + 1) * tok_rows, local_rows), BF16)],
    )
    return combined, token_grad, wgrads[0][None], wgrads[1][None], wgrads[2][None]


def solution(mesh):
    in_specs = (
        P(("dp", "expert"), None),
        P(("dp", "expert"), None),
        P(("dp", "expert"), None),
        P(("dp", "expert"), None),
        P("expert", None, "dp"),
        P("expert", None, "dp"),
        P("expert", "dp", None),
    )
    out_specs = (
        P(("dp", "expert"), None),
        P(("dp", "expert"), None),
        P("expert", None, "dp"),
        P("expert", None, "dp"),
        P("expert", "dp", None),
    )
    return jax.shard_map(local, mesh=mesh, in_specs=in_specs, out_specs=out_specs, check_vma=False)
```

```python
import functools

import jax
import jax.numpy as jnp
from jax import lax
from jax.experimental import pallas as pl
from jax.experimental.pallas import tpu as pltpu
from jax.sharding import PartitionSpec as P

HOT = 4
COLUMNS = 1024
BROAD = 2048
PARTS = 2
STEPS = 2
BF16 = jnp.bfloat16
F32 = jnp.float32
MIB = 1024 * 1024


def dot(left, right, dims):
    return lax.dot_general(left, right, (dims, ((), ())), preferred_element_type=F32)


def swap(value):
    return lax.ppermute(value, "dp", [(0, 1), (1, 0)])


def exchange(value, experts):
    rows, features = value.shape
    parts = value.reshape(experts, rows // experts, features)
    moved = lax.all_to_all(parts, "expert", split_axis=0, concat_axis=0, tiled=True)
    return moved.reshape(rows, features)


def call(kernel, args, outs, limit, grid=(), scratch=(), pinned=False):
    in_specs = [spec for _, spec in args]
    return pl.pallas_call(
        kernel,
        grid=grid,
        in_specs=in_specs,
        out_specs=[spec for _, _, spec in outs],
        out_shape=[
            (pltpu.HBM if pinned and spec.memory_space is None else jax.ShapeDtypeStruct)(shape, kind)
            for shape, kind, spec in outs
        ],
        scratch_shapes=scratch,
        compiler_params=pltpu.CompilerParams(vmem_limit_bytes=limit * MIB),
        cost_estimate=pl.CostEstimate(flops=1000, bytes_accessed=1000, transcendentals=0),
    )(*[arg for arg, _ in args])


def pin(arg):
    return pltpu.with_memory_space_constraint(arg, pltpu.HBM)


def whole(arg):
    return arg, pl.BlockSpec(memory_space=pltpu.VMEM)


def resident(arg):
    return pin(arg), pl.BlockSpec(arg.shape, lambda i: (0, 0), pipeline_mode=pl.Buffered(1))


def fixed(arg):
    return arg, pl.BlockSpec(arg.shape, lambda i: (0, 0))


def across(arg, columns):
    return arg, pl.BlockSpec((arg.shape[0], columns), lambda i: (0, i))


def by_rows(arg, steps):
    return pin(arg), pl.BlockSpec((arg.shape[0] // steps, arg.shape[1]), lambda i: (i, 0))


def out_rows(rows, columns, kind, steps):
    return (rows, columns), kind, pl.BlockSpec((rows // steps, columns), lambda i: (i, 0))


def peer_blocks(peers, steps):
    each = steps // PARTS
    blocks = []
    for part, peer in enumerate(peers):
        index = lambda i, part=part: (jnp.clip(i - part * each, 0, each - 1), 0)
        blocks.append((peer, pl.BlockSpec((peer.shape[0] // each, peer.shape[1]), index)))
    return blocks


def by_column(rows, columns, kind, wide):
    return (rows, columns), kind, pl.BlockSpec((rows, wide), lambda i: (0, i))


def joined(refs):
    return jnp.concatenate([ref[...] for ref in refs], axis=0)


def hidden_parts(rows, gate_matrix, up_matrix):
    gate_pre = dot(rows, gate_matrix, ((1,), (0,)))
    up_pre = dot(rows, up_matrix, ((1,), (0,)))
    sig_gate = jax.nn.sigmoid(gate_pre)
    activated = gate_pre * sig_gate
    hidden = (activated * up_pre).astype(BF16)
    gate_slope = up_pre * sig_gate * (1.0 + gate_pre * (1.0 - sig_gate))
    return hidden, activated, gate_slope


def grad_parts(grads, act, slope, down_matrix):
    hidden_grad = dot(grads, down_matrix, ((1,), (1,)))
    return (hidden_grad * slope).astype(BF16), (hidden_grad * act).astype(BF16)


def input_parts(gate_grad, up_grad, gate_matrix, up_matrix):
    return dot(gate_grad, gate_matrix, ((1,), (1,))) + dot(up_grad, up_matrix, ((1,), (1,)))


def places(routing_ref, position_ref, experts, capacity):
    top_count, tok_rows = routing_ref.shape
    expert_ids = lax.broadcasted_iota(jnp.int32, (experts, tok_rows), 0)
    named = [routing_ref[column : column + 1] == expert_ids for column in range(top_count)]
    counts = sum(hit.astype(F32) for hit in named)
    earlier = lax.broadcasted_iota(jnp.int32, (tok_rows, tok_rows), 0) < lax.broadcasted_iota(
        jnp.int32, (tok_rows, tok_rows), 1
    )
    before = dot(counts.astype(BF16), earlier.astype(F32).astype(BF16), ((1,), (0,)))
    for column, hit in enumerate(named):
        slot = jnp.sum(jnp.where(hit, before, 0.0), axis=0, keepdims=True).astype(jnp.int32)
        position_ref[column : column + 1] = routing_ref[column : column + 1] * capacity + slot


def dispatch_kernel(
    routing_ref, weight_ref, tokens_ref, cotangent_ref, position_ref, kept_ref, rows_ref, grads_ref, pick_ref, scale_ref, *, experts, capacity
):
    @pl.when(pl.program_id(0) == 0)
    def _():
        places(routing_ref, position_ref, experts, capacity)
        kept_ref[...] = weight_ref[...]
        slots = lax.broadcasted_iota(jnp.int32, pick_ref.shape, 0)
        columns = range(position_ref.shape[0])
        hits = [position_ref[column : column + 1] == slots for column in columns]
        pick_ref[...] = sum(hit.astype(F32) for hit in hits).astype(BF16)
        scale = sum(jnp.where(hits[column], weight_ref[column : column + 1], 0.0) for column in columns)
        scale_ref[...] = jnp.broadcast_to(jnp.sum(scale, axis=1, keepdims=True), scale_ref.shape)

    columns = tokens_ref.shape[1]
    here = pl.ds(pl.multiple_of(pl.program_id(0) * columns, columns), columns)
    rows_ref[:, here] = dot(pick_ref[...], tokens_ref[...], ((1,), (0,))).astype(BF16)
    grads = dot(pick_ref[...], cotangent_ref[...], ((1,), (0,)))
    grads_ref[...] = (scale_ref[:, :1] * grads).astype(BF16)


def combine_kernel(position_ref, weight_ref, out_ref, input_ref, combined_ref, token_grad_ref, pick_ref):
    tok_rows, top_count = position_ref.shape

    @pl.when(pl.program_id(0) == 0)
    def _():
        slots = lax.broadcasted_iota(jnp.int32, (tok_rows, pick_ref.shape[1]), 1)
        picks = [(position_ref[:, column : column + 1] == slots).astype(F32) for column in range(top_count)]
        for column, pick in enumerate(picks + [sum(picks)]):
            pick_ref[column * tok_rows : (column + 1) * tok_rows] = pick.astype(BF16)

    found = dot(pick_ref[: top_count * tok_rows], out_ref[...], ((1,), (0,)))
    total = jnp.zeros(combined_ref.shape, F32)
    for column in range(top_count):
        total += weight_ref[:, column : column + 1] * found[column * tok_rows : (column + 1) * tok_rows]
    combined_ref[...] = total.astype(BF16)
    token_grad_ref[...] = dot(pick_ref[top_count * tok_rows :], input_ref[...], ((1,), (0,))).astype(BF16)


def hidden_kernel(rows_ref, gate_ref, up_ref, hidden_ref, act_ref, slope_ref):
    hidden_ref[...], act_ref[...], slope_ref[...] = hidden_parts(rows_ref[...], gate_ref[...], up_ref[...])


def forward_kernel(rows_ref, gate_ref, up_ref, down_ref, hidden_ref, act_ref, slope_ref, *out_refs):
    hidden, act_ref[...], slope_ref[...] = hidden_parts(rows_ref[...], gate_ref[...], up_ref[...])
    hidden_ref[...] = hidden
    out = dot(hidden, down_ref[...], ((1,), (0,))).astype(BF16)
    for i, out_ref in enumerate(out_refs):

        @pl.when(pl.program_id(0) == i)
        def _():
            out_ref[...] = out


def peer_part(peer_refs):
    return jnp.where(pl.program_id(0) < pl.num_programs(0) // PARTS, peer_refs[0][...], peer_refs[1][...]).astype(F32)


def out_kernel(hidden_ref, down_ref, *refs):
    out_ref = refs[-1]
    total = dot(hidden_ref[...], down_ref[...], ((1,), (0,)))
    out_ref[...] = (total + peer_part(refs[:-1])).astype(BF16)


def grad_kernel(grads_ref, act_ref, slope_ref, down_ref, gate_grad_ref, up_grad_ref):
    gate_grad_ref[...], up_grad_ref[...] = grad_parts(grads_ref[...], act_ref[...], slope_ref[...], down_ref[...])


def backward_kernel(grads_ref, act_ref, slope_ref, gate_ref, up_ref, down_ref, gate_grad_ref, up_grad_ref, *in_refs):
    gate_grad, up_grad = grad_parts(grads_ref[...], act_ref[...], slope_ref[...], down_ref[...])
    gate_grad_ref[...] = gate_grad
    up_grad_ref[...] = up_grad
    back = input_parts(gate_grad, up_grad, gate_ref[...], up_ref[...]).astype(BF16)
    for i, in_ref in enumerate(in_refs):

        @pl.when(pl.program_id(0) == i)
        def _():
            in_ref[...] = back


def input_kernel(gate_grad_ref, up_grad_ref, gate_ref, up_ref, *refs):
    out_ref = refs[-1]
    total = input_parts(gate_grad_ref[...], up_grad_ref[...], gate_ref[...], up_ref[...])
    rows = total.shape[0]
    out_ref[pl.ds(pl.multiple_of(pl.program_id(0) * rows, rows), rows)] = (total + peer_part(refs[:-1])).astype(BF16)


def weight_kernel(*refs):
    rows, grads, hidden, gate_grad, up_grad = (refs[2 * i : 2 * i + 2] for i in range(5))
    gate_out, up_out, down_out = refs[10:]
    both = jnp.concatenate([joined(gate_grad), joined(up_grad)], axis=1)
    total = dot(joined(rows), both, ((0,), (0,)))
    width = gate_out.shape[1]
    gate_out[...] = total[:, :width].astype(BF16)
    up_out[...] = total[:, width:].astype(BF16)
    down_out[...] = dot(joined(hidden), joined(grads), ((0,), (0,))).astype(BF16)


def weight_grads(wide, kept):
    features = wide[0].shape[1]
    width = kept[0].shape[1]
    args = [across(pin(value), COLUMNS) for value in wide] + [fixed(pin(value)) for value in kept]
    tall = ((features, width), BF16, pl.BlockSpec((COLUMNS, width), lambda i: (i, 0)))
    return call(weight_kernel, args, [tall, tall, by_column(width, features, BF16, COLUMNS)], 48, grid=(features // COLUMNS,))


def local(tokens, cotangent, routing, combine_weights, w_gate, w_up, w_down):
    tok_rows, features = tokens.shape
    top_count = routing.shape[1]
    experts = lax.axis_size("expert")
    cold_count = experts - HOT
    hot_cap = 2 * tok_rows * top_count // experts
    cold_cap = (tok_rows * top_count - HOT * hot_cap + cold_count - 1) // cold_count
    capacity = max(hot_cap, cold_cap)
    local_rows = experts * capacity
    gate_matrix, up_matrix, down_matrix = w_gate[0], w_up[0], w_down[0]
    width = gate_matrix.shape[1]
    broad_grid = (features // BROAD,)
    place_shape = (top_count, tok_rows)
    sent = by_column(local_rows, features, BF16, BROAD)
    position, route_weights, send_rows, send_grads = call(
        functools.partial(dispatch_kernel, experts=experts, capacity=capacity),
        [fixed(pin(routing.T)), fixed(pin(combine_weights.T)), across(pin(tokens), BROAD), across(pin(cotangent), BROAD)],
        [(place_shape, kind, pl.BlockSpec(place_shape, lambda i: (0, 0))) for kind in (jnp.int32, F32)] + [((local_rows, features), BF16, pl.BlockSpec(memory_space=pltpu.VMEM)), sent],
        40,
        grid=broad_grid,
        scratch=[pltpu.VMEM((local_rows, tok_rows), BF16), pltpu.VMEM((local_rows, 128), F32)],
        pinned=True,
    )
    rows_own = exchange(send_rows, experts)
    rows_own, send_grads, position, route_weights = lax.optimization_barrier(
        (rows_own, send_grads, position, route_weights)
    )
    position, route_weights = position.T, route_weights.T
    grads_own = exchange(send_grads, experts)

    weights = [whole(matrix) for matrix in (gate_matrix, up_matrix, down_matrix)]
    own_weights = [resident(matrix) for matrix in (gate_matrix, up_matrix, down_matrix)]
    kept = [out_rows(local_rows, width, kind, PARTS) for kind in (BF16, F32, F32)]
    pair = [out_rows(local_rows, width, BF16, PARTS)] * 2
    part = (local_rows // PARTS, features)
    parts = [(part, BF16, pl.BlockSpec(part, lambda i: (0, 0)))] * PARTS
    send = [out_rows(local_rows, features, BF16, STEPS)]
    halves = dict(grid=(PARTS,), pinned=True)
    steps = dict(grid=(STEPS,), pinned=True)

    rows_peer = swap(rows_own)
    hidden_own, act_own, slope_own = call(hidden_kernel, [by_rows(rows_own, PARTS)] + weights[:2], kept, 32, **halves)
    hidden_peer, act_peer, slope_peer, *outs = call(
        forward_kernel, [by_rows(rows_peer, PARTS)] + weights, kept + parts, 44, **halves
    )
    outs = [swap(out) for out in outs]
    (out_send,) = call(
        out_kernel, [by_rows(hidden_own, STEPS)] + weights[2:] + peer_blocks(outs, STEPS), send, 32, **steps
    )
    grads_own, out_send = lax.optimization_barrier((grads_own, out_send))
    out_back = exchange(out_send, experts)

    grads_peer = swap(grads_own)
    gate_own, up_own = call(
        grad_kernel,
        [by_rows(value, PARTS) for value in (grads_own, act_own, slope_own)] + weights[2:],
        pair,
        32,
        **halves,
    )
    gate_peer, up_peer, *ins = call(
        backward_kernel,
        [by_rows(value, PARTS) for value in (grads_peer, act_peer, slope_peer)] + own_weights,
        pair + parts,
        44,
        **halves,
    )
    ins = [swap(value) for value in ins]
    (input_send,) = call(
        input_kernel,
        [by_rows(gate_own, STEPS), by_rows(up_own, STEPS)] + weights[:2] + peer_blocks(ins, STEPS),
        [((local_rows, features), BF16, pl.BlockSpec(memory_space=pltpu.VMEM))],
        32,
        **steps,
    )
    wgrads = weight_grads(
        [rows_own, rows_peer, grads_own, grads_peer],
        [hidden_own, hidden_peer, gate_own, gate_peer, up_own, up_peer],
    )
    out_back, input_send, position, route_weights, *wgrads = lax.optimization_barrier(
        (out_back, input_send, position, route_weights, *wgrads)
    )
    input_back = exchange(input_send, experts)
    combined, token_grad = call(
        combine_kernel,
        [fixed(position), fixed(route_weights), across(out_back, BROAD), across(input_back, BROAD)],
        [by_column(tok_rows, features, BF16, BROAD)] * 2,
        40,
        grid=broad_grid,
        scratch=[pltpu.VMEM(((top_count + 1) * tok_rows, local_rows), BF16)],
    )
    return combined, token_grad, wgrads[0][None], wgrads[1][None], wgrads[2][None]


def solution(mesh):
    in_specs = (
        P(("dp", "expert"), None),
        P(("dp", "expert"), None),
        P(("dp", "expert"), None),
        P(("dp", "expert"), None),
        P("expert", None, "dp"),
        P("expert", None, "dp"),
        P("expert", "dp", None),
    )
    out_specs = (
        P(("dp", "expert"), None),
        P(("dp", "expert"), None),
        P("expert", None, "dp"),
        P("expert", None, "dp"),
        P("expert", "dp", None),
    )
    return jax.shard_map(local, mesh=mesh, in_specs=in_specs, out_specs=out_specs, check_vma=False)
```
